256 devices in a mesh: sweep: 8 (over x, z_lo), op: 32 (over z_hi, y, core).
Axes of the slice: x: 4, y: 4, z: 8 (z_hi: 4, z_lo: 2; z = z_hi * 2 + z_lo), core: 2. Of those that a mesh axis runs over, the one named last changes fastest.
Arguments:
- environment: bfloat16 [128, 4, 256, 256], P('op'), may hold values from -6 to 6
- rotations: bfloat16 [16, 4, 256, 1024], P('sweep', None, 'op'), may hold values from -0.25 to 0.25
- site_terms: bfloat16 [16, 4, 256, 256], P('sweep', None, 'op'), may hold values from -6 to 6
- pair_of: int32 [128], P('op'), may hold values from 0 to 2079
- targets: int32 [128, 4], P('op'), may hold values from 0 to 3
- coupling: float32 [16, 2080], P('sweep'), may hold values from -1 to 1
- energy_coef: float32 [16, 2080], P('sweep'), may hold values from -0.25 to 0.25
Outputs:
- renormalized: bfloat16 [8, 128, 4, 256, 256], P('sweep', 'op')
- energies: float32 [16, 4, 256, 256], P('sweep')
The draws below stay inside these ranges and needn't reach their ends.
All inputs are finite; a program needn't handle non-finite values.
Results may differ from the reference program's by a relative error of at most 0.025.
Values may be sent and summed in bfloat16 or wider, within the bound.
No kernel may reach another device: no remote copies, remote signals or barrier semaphores. Data moves between devices by JAX's collectives and lax.ppermute only.
A program may use at most 128 MiB of HBM per device.

```python
import jax
import jax.numpy as jnp
from jax import lax

SECT = 4
BLK = 256
LOCAL = 4
PAIRS = 2080
SITES_DEV = 2
OPS = 128
SITES = 16


def touch_ends(result, rng, least, largest):
    extent = result.shape
    place = [jax.random.randint(jax.random.fold_in(rng, axis), (), 0, extent[axis]) for axis in range(len(extent))]
    result = result.at[tuple(place)].set(least)
    longest = extent.index(max(extent))
    place[longest] = (place[longest] + 1) % extent[longest]
    return result.at[tuple(place)].set(largest)


def block_levels(own_key, shape, cuts, least, top_value):
    factor_of = 1.0
    for position, shards_of in cuts:
        steps = jax.random.uniform(jax.random.fold_in(jax.random.fold_in(own_key, 6), position), (shards_of,), jnp.float32, least / len(cuts), top_value / len(cuts))
        factor_of = factor_of * jnp.repeat(jnp.exp(steps), shape[position] // shards_of).reshape((-1,) + (1,) * (len(shape) - 1 - position))
    return factor_of


def normal_values(key, dims, width, limit, shards=(), held_as=jnp.bfloat16):
    array = jax.random.normal(key, dims, jnp.float32) * width
    if len(shards) > 0:
        array = block_levels(key, dims, shards, -0.22, 0.18) * array
    return jnp.clip(array, min=-limit, max=limit).astype(held_as)


def setup_inputs(seed: int = 0) -> dict:
    seeds = jax.random.split(jax.random.key(seed), 8)
    environment = normal_values(seeds[0], (OPS, SECT, BLK, BLK), 1.0, 6.0, ((0, 32),))
    rotations = normal_values(seeds[1], (SITES, SECT, BLK, LOCAL * BLK), (2 * BLK) ** -0.5, 0.25, ((0, 8), (2, 32)))
    site_terms = normal_values(seeds[2], (SITES, SECT, BLK, BLK), 1.0, 6.0, ((0, 8), (2, 32)))
    pair_of = touch_ends(jax.random.randint(seeds[3], (OPS,), 0, PAIRS), jax.random.fold_in(seeds[3], 1), 0, PAIRS - 1).astype(jnp.int32)
    targets = touch_ends(jax.random.randint(seeds[4], (OPS, SECT), 0, SECT), jax.random.fold_in(seeds[4], 1), 0, SECT - 1).astype(jnp.int32)
    coupling = jnp.clip(jax.random.uniform(seeds[5], (SITES, PAIRS), jnp.float32, -1.0, 1.0) * block_levels(seeds[5], (SITES, PAIRS), ((0, 8),), -0.4, 0.0), -1.0, 1.0)
    energy_coef = jnp.clip(jax.random.uniform(seeds[6], (SITES, PAIRS), jnp.float32, -0.25, 0.25) * block_levels(seeds[6], (SITES, PAIRS), ((0, 8),), -0.4, 0.0), -0.25, 0.25)
    return dict(environment=environment, rotations=rotations, site_terms=site_terms, pair_of=pair_of, targets=targets, coupling=coupling, energy_coef=energy_coef)


def renormalize(operator, rotation, site_term, target, coupling_value):
    right_rows = jnp.take(rotation, target, axis=0)
    middle = jnp.einsum('sxa,sac->sxc', operator.astype(jnp.float32), right_rows.astype(jnp.float32)).astype(jnp.bfloat16)
    sectors, block_size = operator.shape[0], operator.shape[-1]
    local_states = rotation.shape[-1] // block_size
    left_rows = rotation.reshape(sectors, block_size, local_states, block_size)
    middle_rows = middle.reshape(sectors, block_size, local_states, block_size)
    rotated = jnp.einsum('sxdb,sxdc->sbc', left_rows.astype(jnp.float32), middle_rows.astype(jnp.float32))
    return (rotated + coupling_value * site_term.astype(jnp.float32)).astype(jnp.bfloat16)


def reference(environment, rotations, site_terms, pair_of, targets, coupling, energy_coef):
    current = environment
    stored = []
    energies = []
    for site_num in range(SITES):
        couplings = coupling[site_num][pair_of]
        weights_here = energy_coef[site_num][pair_of]

        def advance(operands):
            operator, target, coupling_value = operands
            return renormalize(operator, rotations[site_num], site_terms[site_num], target, coupling_value)

        current = lax.map(advance, (current, targets, couplings))
        energies.append(jnp.sum(weights_here[:, None, None, None] * current.astype(jnp.float32), axis=0))
        if site_num % SITES_DEV == SITES_DEV - 1:
            stored.append(current)
    return jnp.stack(stored), jnp.stack(energies)
```

```python
import functools

import jax
import jax.numpy as jnp
from jax import lax
from jax.experimental import pallas as pl
from jax.experimental.pallas import tpu as pltpu
from jax.sharding import PartitionSpec as P

NX, NZL, NZH, NY, NC = 4, 2, 4, 4, 2
NZ = NZL * NZH
SECT, BLK, LOCAL = 4, 256, 4
WIDE = LOCAL * BLK
BOTH = WIDE + BLK
ITEMS = 8
LAG = 2
TICKS = ITEMS + LAG * (NX - 1)
VMEM_LIMIT = 48 * 1024 * 1024

AXES = ("sweep", "op")
Z_ORDER = (0, -1, -2, -3, 4, 3, 2, 1)
Y_ORDER = (0, -1, 2, 1)


def number(x, z, y, c):
    zh, zl = z // 2, z % 2
    return (x * NZL + zl) * (NZH * NY * NC) + (zh * NY + y) * NC + c


def send(value, rule):
    pairs = []
    for x in range(NX):
        for z in range(NZ):
            for y in range(NY):
                for c in range(NC):
                    to = rule(x, z, y, c)
                    if to is not None:
                        pairs.append((number(x, z, y, c), number(*to)))
    return lax.ppermute(value, AXES, pairs)


def along_y(value, step):
    return send(value, lambda x, z, y, c: (x, z, (y + step) % NY, c))


def along_z(value, step):
    return send(value, lambda x, z, y, c: (x, (z + step) % NZ, y, c))


def other_core(value):
    return send(value, lambda x, z, y, c: (x, z, y, 1 - c))


def other_lane(value):
    return send(value, lambda x, z, y, c: (x, z ^ 1, y, c))


def next_stage(value):
    return send(value, lambda x, z, y, c: (x + 1, z, y, c) if x + 1 < NX else None)


def gather_plane(block):
    first, second = block[:2], block[2:]
    below, above = along_y(first, 1), along_y(first, -1)
    far = jnp.concatenate([along_y(below[:1], 1), along_y(above[1:], -1)])
    rows = jnp.stack([first, below, far, above])
    down, up = [second], [second]
    rdown, rup = [rows], [rows]
    for _ in range(3):
        down.append(along_z(down[-1], 1))
        up.append(along_z(up[-1], -1))
        rdown.append(along_z(rdown[-1], 1))
        rup.append(along_z(rup[-1], -1))
    opposite = jnp.concatenate([along_z(down[3][:1], 1), along_z(up[3][1:], -1)])
    column = jnp.stack([second, down[1], down[2], down[3], opposite, up[3], up[2], up[1]])
    ropp = [along_z(rdown[3][:2], 1), along_z(rup[3][2:], -1)]
    cbelow, cabove = along_y(column, 1), along_y(column, -1)
    cfar = [along_y(cbelow[:4], 1), along_y(cabove[4:], -1)]
    return [rows, rdown[1], rdown[2], rdown[3], ropp[0], ropp[1], rup[3], rup[2], rup[1], column, cbelow, cfar[0], cfar[1], cabove]


def assemble_kernel(place, *refs):
    pieces = refs[:28]
    rot, left, site = refs[28:]
    z, y, c, zl = place[0], place[1], place[2], place[3]

    def put(ref, lead, sector, dz, dy, core):
        zs = lax.rem(z + (dz + NZ), NZ)
        ys = lax.rem(y + (dy + NY), NY)
        at = 2 * lax.rem(zs, 2) + core
        row = pl.multiple_of(((zs // 2) * NY + ys) * 16, 16)
        for i in range(2):
            rot[at, sector + i, pl.ds(row, 16), :] = ref[lead, i, :, :WIDE]

        @pl.when(zl == sector // 2)
        def _():
            for i in range(2):
                site[at, i, pl.ds(row, 16), :] = ref[lead, i, :, WIDE:]

    for which in range(2):
        core = c if which == 0 else 1 - c
        part = pieces[14 * which : 14 * which + 14]
        lines = {0: part[0], -1: part[1], -2: part[2], -3: part[3], 3: part[6], 2: part[7], 1: part[8]}
        for dz, ref in lines.items():
            for n, dy in enumerate(Y_ORDER):
                put(ref, n, 0, dz, dy, core)
        for n, dy in enumerate(Y_ORDER):
            put(part[4 + n // 2], n % 2, 0, 4, dy, core)
        for dy, ref in {0: part[9], -1: part[10], 1: part[13]}.items():
            for n, dz in enumerate(Z_ORDER):
                put(ref, n, 2, dz, dy, core)
        for n, dz in enumerate(Z_ORDER):
            put(part[11 + n // 4], n % 4, 2, dz, 2, core)

    def turn(n, _):
        at, own = n // 2, lax.rem(n, 2)
        for d in range(LOCAL):
            cols = slice(d * BLK, (d + 1) * BLK)
            left[at, own, :, cols] = rot[at, 2 * zl + own, :, cols].T
        return _

    lax.fori_loop(0, 8, turn, 0)


def assemble(place, pieces):
    vmem = pl.BlockSpec(memory_space=pltpu.VMEM)
    return pl.pallas_call(
        assemble_kernel,
        out_shape=(
            jax.ShapeDtypeStruct((4, SECT, BLK, WIDE), jnp.bfloat16),
            jax.ShapeDtypeStruct((4, 2, BLK, WIDE), jnp.bfloat16),
            jax.ShapeDtypeStruct((4, 2, BLK, BLK), jnp.bfloat16),
        ),
        in_specs=[pl.BlockSpec(memory_space=pltpu.SMEM)] + [vmem] * len(pieces),
        out_specs=(vmem, vmem, vmem),
        compiler_params=pltpu.CompilerParams(vmem_limit_bytes=VMEM_LIMIT),
        name="assemble",
    )(place, *pieces)


def item_of(tick, x):
    return jnp.clip(tick - LAG * x, 0, ITEMS - 1)


def step_kernel(tick, meta, consts, env, arrived, swapped, rot, left, site, e_in, out_in, e_out, out, hop, swap, current, keep, sem):
    del out_in
    s = pl.program_id(0)
    x, zl = meta[0], meta[1]
    turn = tick - LAG * x
    valid = (turn >= 0) & (turn < ITEMS)
    item = item_of(tick, x)
    k, own = lax.rem(item, 4), item // 4
    before = turn - LAG
    known = (before >= 0) & (before < ITEMS)
    past = jnp.clip(before, 0, ITEMS - 1)
    copy_past = pltpu.make_async_copy(swapped, out.at[lax.rem(past, 4), 2 * (1 - zl) + past // 4], sem.at[1])
    copy_keep = pltpu.make_async_copy(keep, out.at[k, 2 * zl + own], sem.at[0])

    @pl.when((s == 0) & known)
    def _():
        copy_past.start()

    @pl.when((s == 0) & (x == 0))
    def _():
        current[...] = env[0, 0]

    @pl.when((s == 0) & (x != 0))
    def _():
        current[...] = arrived[...]

    @pl.when(valid)
    def _():
        middle = jnp.dot(current[...], rot[0, 0], preferred_element_type=jnp.float32).astype(jnp.bfloat16)
        total = consts[s, k] * site[0, 0].astype(jnp.float32)
        for d in range(LOCAL):
            cols = slice(d * BLK, (d + 1) * BLK)
            total += jnp.dot(left[0, 0, :, cols], middle[:, cols], preferred_element_type=jnp.float32)
        new = total.astype(jnp.bfloat16)
        current[...] = new
        e_out[0, 0] = e_in[0, 0] + consts[4 + s, k] * new.astype(jnp.float32)

        @pl.when(s == 1 + 2 * zl)
        def _():
            keep[...] = new
            copy_keep.start()

        @pl.when(s == 3 - 2 * zl)
        def _():
            swap[...] = new

        @pl.when(s == 3)
        def _():
            hop[...] = new
            copy_keep.wait()

    @pl.when(jnp.logical_not(valid))
    def _():
        e_out[0, 0] = e_in[0, 0]

    @pl.when((s == 3) & known)
    def _():
        copy_past.wait()


def step(tick, meta, consts, env, arrived, swapped, rot, left, site, energy, out):
    def where(f):
        def index(s, meta):
            x, zl = meta[0], meta[1]
            item = item_of(tick, x)
            k, own = lax.rem(item, 4), item // 4
            return f(s, k, own, 2 * zl + own, meta)

        return index

    tile = jax.ShapeDtypeStruct((BLK, BLK), jnp.bfloat16)
    whole = pl.BlockSpec((BLK, BLK), lambda s, meta: (0, 0))
    anywhere = pl.BlockSpec(memory_space=pl.ANY)
    per_site = pl.BlockSpec((1, 1, BLK, BLK), where(lambda s, k, own, sec, meta: (own, s, 0, 0)))
    return pl.pallas_call(
        functools.partial(step_kernel, tick),
        grid_spec=pltpu.PrefetchScalarGridSpec(
            num_scalar_prefetch=1,
            grid=(4,),
            in_specs=[
                pl.BlockSpec(memory_space=pltpu.SMEM),
                pl.BlockSpec((1, 1, BLK, BLK), where(lambda s, k, own, sec, meta: (k, sec, 0, 0))),
                whole,
                anywhere,
                pl.BlockSpec((1, 1, BLK, WIDE), where(lambda s, k, own, sec, meta: (s, meta[2 + 4 * k + sec], 0, 0))),
                pl.BlockSpec((1, 1, BLK, WIDE), where(lambda s, k, own, sec, meta: (s, own, 0, 0))),
                pl.BlockSpec((1, 1, BLK, BLK), where(lambda s, k, own, sec, meta: (s, own, 0, 0))),
                per_site,
                anywhere,
            ],
            out_specs=[per_site, anywhere, whole, whole],
            scratch_shapes=[
                pltpu.VMEM((BLK, BLK), jnp.bfloat16),
                pltpu.VMEM((BLK, BLK), jnp.bfloat16),
                pltpu.SemaphoreType.DMA((2,)),
            ],
        ),
        out_shape=(
            jax.ShapeDtypeStruct(energy.shape, energy.dtype),
            jax.ShapeDtypeStruct(out.shape, out.dtype),
            tile,
            tile,
        ),
        input_output_aliases={8: 0, 9: 1},
        compiler_params=pltpu.CompilerParams(vmem_limit_bytes=VMEM_LIMIT, dimension_semantics=("arbitrary",)),
        cost_estimate=pl.CostEstimate(flops=4 * 4 * BLK * BLK * WIDE, bytes_accessed=8 << 20, transcendentals=0),
        name="renormalize",
    )(meta, consts, env, arrived, swapped, rot, left, site, energy, out)


def finish_kernel(meta, first, second, out_in, out, sem):
    del out_in
    x, zl = meta[0], meta[1]
    copies = []
    for n, ref in enumerate((first, second)):
        item = TICKS - LAG + n - LAG * x
        known = (item >= 0) & (item < ITEMS)
        past = jnp.clip(item, 0, ITEMS - 1)
        copy = pltpu.make_async_copy(ref, out.at[lax.rem(past, 4), 2 * (1 - zl) + past // 4], sem.at[n])
        copies.append((known, copy))
        pl.when(known)(copy.start)
    for known, copy in copies:
        pl.when(known)(copy.wait)


def finish(meta, first, second, out):
    anywhere = pl.BlockSpec(memory_space=pl.ANY)
    return pl.pallas_call(
        finish_kernel,
        in_specs=[pl.BlockSpec(memory_space=pltpu.SMEM)] + [anywhere] * 3,
        out_specs=anywhere,
        out_shape=jax.ShapeDtypeStruct(out.shape, out.dtype),
        scratch_shapes=[pltpu.SemaphoreType.DMA((2,))],
        input_output_aliases={3: 0},
        name="finish",
    )(meta, first, second, out)


def piece(value, axis, place, size):
    return lax.dynamic_slice_in_dim(value, place * size, size, axis)


def spread(value, axis, place, rule):
    size = value.shape[axis] // 4
    total = piece(value, axis, place, size)
    for step_ in (1, -1, 2):
        part = piece(value, axis, (place + step_) % 4, size).astype(jnp.bfloat16)
        total = total + rule(part, step_).astype(jnp.float32)
    return total


def collect(value, axis, place, rule):
    size = value.shape[axis]
    parts = {0: value}
    for step_ in (1, -1, 2):
        parts[(-step_) % 4] = rule(value, step_)
    line = jnp.concatenate([parts[n] for n in (0, 1, 2, 3, 0, 1, 2)], axis=axis)
    return lax.dynamic_slice_in_dim(line, ((4 - place) % 4) * size, 4 * size, axis)


def reduce_energy(energy, zl, zh, y, c):
    def along_zh(value, step_):
        return along_z(value, 2 * step_)

    half = BLK // 2
    theirs = piece(energy, 2, 1 - c, half).astype(jnp.bfloat16)
    total = piece(energy, 2, c, half) + other_core(theirs).astype(jnp.float32)
    total = spread(total, 2, y, along_y)
    total = spread(total, 2, zh, along_zh)
    total = total.astype(jnp.bfloat16)
    mine, theirs = piece(total, 1, zl, 2), piece(total, 1, 1 - zl, 2)
    got = other_lane(theirs)
    flat = jnp.where(zl == 0, jnp.concatenate([mine, got]), jnp.concatenate([got, mine])).swapaxes(0, 1)
    flat = collect(flat, 2, zh, along_zh)
    flat = collect(flat, 2, y, along_y)
    got = other_core(flat)
    flat = jnp.where(c == 0, jnp.concatenate([flat, got], axis=2), jnp.concatenate([got, flat], axis=2))
    return flat.astype(jnp.float32)


def local(environment, rotations, site_terms, pair_of, targets, coupling, energy_coef):
    sweep, op = lax.axis_index("sweep"), lax.axis_index("op")
    x, zl = sweep // 2, sweep % 2
    zh, y, c = op // 8, (op // 2) % 4, op % 2
    z = 2 * zh + zl

    wide = jnp.concatenate([rotations, site_terms], axis=3)
    mine, theirs = wide[c], wide[1 - c]
    got = other_core(theirs)
    block = jnp.where(c == 0, jnp.concatenate([mine, got], axis=1), jnp.concatenate([got, mine], axis=1))
    pieces = gather_plane(block)
    shared = [other_core(p) for p in pieces]
    place = jnp.stack([z, y, c, zl]).astype(jnp.int32)
    rot, left, site = assemble(place, pieces + shared)

    values = jnp.stack([jnp.take(coupling, pair_of, axis=1), jnp.take(energy_coef, pair_of, axis=1)])
    got = other_lane(values)
    consts = jnp.where(zl == 0, jnp.concatenate([values, got], axis=1), jnp.concatenate([got, values], axis=1)).reshape(8, 4)
    meta = jnp.concatenate([jnp.stack([x, zl]).astype(jnp.int32), targets.reshape(-1)])

    energy = jnp.zeros((2, 4, BLK, BLK), jnp.float32)
    out = jnp.zeros(environment.shape, jnp.bfloat16)
    blank = jnp.zeros((BLK, BLK), jnp.bfloat16)
    hops, swaps = [], []
    for tick in range(TICKS):
        arrived = hops[tick - LAG] if tick >= LAG else blank
        swapped = swaps[tick - LAG] if tick >= LAG else blank
        energy, out, hop, swap = step(tick, meta, consts, environment, arrived, swapped, rot, left, site, energy, out)
        hops.append(next_stage(hop) if tick < TICKS - LAG else None)
        swaps.append(other_lane(swap))
    out = finish(meta, swaps[-2], swaps[-1], out)
    return out[None], reduce_energy(energy, zl, zh, y, c)


def solution(mesh):
    return jax.shard_map(
        local,
        mesh=mesh,
        in_specs=(
            P("op", None, None, None),
            P("sweep", None, "op", None),
            P("sweep", None, "op", None),
            P("op"),
            P("op", None),
            P("sweep", None),
            P("sweep", None),
        ),
        out_specs=(P("sweep", "op", None, None, None), P("sweep", None, None, None)),
        check_vma=False,
    )
```

```python
import functools

import jax
import jax.numpy as jnp
from jax import lax
from jax.experimental import pallas as pl
from jax.experimental.pallas import tpu as pltpu
from jax.sharding import PartitionSpec as P

NX, NZL, NZH, NY, NC = 4, 2, 4, 4, 2
NZ = NZL * NZH
SECT, BLK, LOCAL = 4, 256, 4
WIDE = LOCAL * BLK
BOTH = WIDE + BLK
ITEMS = 8
LAG = 2
TICKS = ITEMS + LAG * (NX - 1)
STEP_LIMIT = 8 * 1024 * 1024

FIRST_AXES = (((0,), (0,)), ((), ()))
AXES = ("sweep", "op")


def number(x, z, y, c):
    zh, zl = z // 2, z % 2
    return (x * NZL + zl) * (NZH * NY * NC) + (zh * NY + y) * NC + c


def send(value, rule):
    pairs = []
    for x in range(NX):
        for z in range(NZ):
            for y in range(NY):
                for c in range(NC):
                    to = rule(x, z, y, c)
                    if to is not None:
                        pairs.append((number(x, z, y, c), number(*to)))
    return lax.ppermute(value, AXES, pairs)


def along_y(value, step):
    return send(value, lambda x, z, y, c: (x, z, (y + step) % NY, c))


def along_z(value, step):
    return send(value, lambda x, z, y, c: (x, (z + step) % NZ, y, c))


def other_core(value):
    return send(value, lambda x, z, y, c: (x, z, y, 1 - c))


def other_lane(value):
    return send(value, lambda x, z, y, c: (x, z ^ 1, y, c))


def next_stage(value):
    return send(value, lambda x, z, y, c: (x + 1, z, y, c) if x + 1 < NX else None)


def after(value, *others):
    return lax.optimization_barrier((value, others))[0]


def held(value):
    return pltpu.with_memory_space_constraint(value, pltpu.VMEM)


def piece_copies(layout, place, pieces, rot, site, sem):
    z, y, c, zl = place[0], place[1], place[2], place[3]
    copies = []
    for n, (ref, (source, other, near, wide)) in enumerate(zip(pieces, layout)):
        if source is None:
            core, does = (1 - c if other else c), None
            dz = [jnp.where(core == 0, p[0], q[0]) for p, q in zip(near, wide)]
            dy = [jnp.where(core == 0, p[1], q[1]) for p, q in zip(near, wide)]
        else:
            core, does = source, c == (1 - source if other else source)
            dz, dy = [p[0] for p in near], [p[1] for p in near]
        for lead in range(len(near)):
            zs = lax.rem(z + NZ + dz[lead], NZ)
            ys = lax.rem(y + NY + dy[lead], NY)
            at = 2 * lax.rem(zs, 2) + core
            row = pl.ds(pl.multiple_of(((zs // 2) * NY + ys) * 16, 16), 16)
            some = ref.at[lead, pl.ds(2 * zl, 2), :, pl.ds(WIDE, BLK)]
            all_ = ref.at[lead, :, :, pl.ds(0, WIDE)]
            copies.append((does, pltpu.make_async_copy(all_, rot.at[at, :, row, :], sem.at[n, lead, 0])))
            copies.append((does, pltpu.make_async_copy(some, site.at[at, :, row, :], sem.at[n, lead, 1])))
    return copies


def run_all(copies):
    for does, copy in copies:
        if does is None:
            copy.start()
        else:
            pl.when(does)(copy.start)
    for does, copy in copies:
        if does is None:
            copy.wait()
        else:
            pl.when(does)(copy.wait)


def put_kernel(layout, place, *refs):
    rot, site, sem = refs[-3:]
    run_all(piece_copies(layout, place, refs[: len(layout)], rot, site, sem))


def load_kernel(layout, place, *refs):
    pieces, (rot_in, site_in, rot, site, sem, whole) = refs[: len(layout)], refs[len(layout) :]
    run_all([(None, pltpu.make_async_copy(rot_in, rot, whole.at[0])), (None, pltpu.make_async_copy(site_in, site, whole.at[1]))])
    run_all(piece_copies(layout, place, pieces, rot, site, sem))


def put(place, pieces, into, last=False):
    layout = [where for _, where in pieces]
    values = [value for value, _ in pieces]
    count = len(pieces)
    vmem, hbm = pl.BlockSpec(memory_space=pltpu.VMEM), pl.BlockSpec(memory_space=pltpu.HBM)
    shapes = [(4, SECT, BLK, WIDE), (4, 2, BLK, BLK)]
    extra = [] if into is None else list(into)
    sems = [pltpu.SemaphoreType.DMA((count, 4, 2))]
    if last:
        sems.append(pltpu.SemaphoreType.DMA((2,)))
    kind = pltpu.VMEM if last else pltpu.HBM
    return pl.pallas_call(
        functools.partial(load_kernel if last else put_kernel, layout),
        out_shape=tuple(kind(shape, jnp.bfloat16) for shape in shapes),
        in_specs=[pl.BlockSpec(memory_space=pltpu.SMEM)] + [vmem] * count + [hbm] * len(extra),
        out_specs=(vmem if last else hbm,) * 2,
        scratch_shapes=sems,
        input_output_aliases={} if into is None or last else {1 + count: 0, 2 + count: 1},
        compiler_params=pltpu.CompilerParams(vmem_limit_bytes=STEP_LIMIT),
        name="load" if last else "put",
    )(place, *values, *extra)


def by_core(value, near, wide):
    def rule(x, z, y, c):
        move = near if c == 0 else wide
        if move is None:
            return None
        return x, (z + move[0]) % NZ, (y + move[1]) % NY, c

    return send(value, rule)


def gather_plane(block, place, extra):
    together = lax.optimization_barrier
    up, down, right, left = (1, 0), (-1, 0), (0, 1), (0, -1)
    up2, down2, right2 = (2, 0), (-2, 0), (0, 2)
    near = [by_core(block, right, up), by_core(block, left, down), by_core(block, right2, up2), by_core(block, None, down2)]
    (lower, upper, lower2, upper2), extra = together((tuple(near), extra))
    head = jnp.stack([block, lower, lower2, upper])
    lead, lag = by_core(head, up, right), by_core(head, down, left)
    lower34, upper3 = by_core(head[1:3], None, up2), by_core(upper, None, down2)
    head_shared = other_core(head)
    lead, lag = together((lead, lag))

    lead2, lag2 = by_core(lead, up, right), by_core(lag, down, None)
    tail = jnp.concatenate([lower34, upper2[None], upper3[None]])
    lead_shared, lag_shared = other_core(lead), other_core(lag)
    lead2, lag2, tail = together((lead2, lag2, tail))
    third, fourth = jnp.where(place[2] == 0, lead2, tail), jnp.where(place[2] == 0, lag2, tail)
    third, fourth = together((third, fourth))

    lead3, lag3 = by_core(third, up, right), by_core(fourth, down, left)
    tail_shared, lead2_shared, lag2_shared = core_to_core(tail, 1), other_core(lead2), core_to_core(lag2, 0)
    ready = [(head, HEAD), (lead, LEAD), (lag, LAG1)]
    ready += [(head_shared, from_other(HEAD)), (lead_shared, from_other(LEAD)), (lag_shared, from_other(LAG1))]
    into = put(place, ready, None)
    lead3, lag3, into = together((lead3, lag3, into))

    far = by_core(lead3[:2], up, right), by_core(lag3[2:], down, left)
    lead3_shared, lag3_shared = other_core(lead3), other_core(lag3)
    ready = [(lead2, LEAD2), (lag2, LAG2), (tail, TAIL)]
    ready += [(lead2_shared, from_other(LEAD2)), (lag2_shared, from_other(LAG2)), (tail_shared, from_other(TAIL))]
    into = put(place, ready, into)
    far, into = together((far, into))
    ready = [(lead3, LEAD3), (lag3, LAG3), (lead3_shared, from_other(LEAD3)), (lag3_shared, from_other(LAG3))]
    for n in range(2):
        ready += [(far[n], FAR[n]), (other_core(far[n]), from_other(FAR[n]))]
    return *put(place, ready, into, True), extra


def core_to_core(value, source):
    return send(value, lambda x, z, y, c: (x, z, y, 1 - c) if c == source else None)


def rows_at(dz):
    return [(dz, dy) for dy in (0, -1, 2, 1)]


def column_at(dy, zs):
    return [(dz, dy) for dz in zs]


def from_other(where):
    return (where[0], True, *where[2:])


Z_HEAD, Z_TAIL = (0, -1, -2, 1), (-3, 4, 2, 3)
HEAD = (None, False, rows_at(0), column_at(0, Z_HEAD))
LEAD = (None, False, rows_at(-1), column_at(-1, Z_HEAD))
LAG1 = (None, False, rows_at(1), column_at(1, Z_HEAD))
LEAD2 = (None, False, rows_at(-2), column_at(2, Z_HEAD))
LAG2 = (0, False, rows_at(2), None)
LEAD3 = (None, False, rows_at(-3), column_at(-1, Z_TAIL))
LAG3 = (None, False, rows_at(3), column_at(1, Z_TAIL))
TAIL = (1, False, column_at(0, Z_TAIL), None)
FAR = tuple((None, False, rows_at(4)[n : n + 2], column_at(2, Z_TAIL)[n : n + 2]) for n in (0, 2))


def item_of(tick, x):
    return jnp.clip(tick - LAG * x, 0, ITEMS - 1)


def step_kernel(tick, meta, consts, env, *refs):
    refs = list(refs)
    arrived = refs.pop(0) if tick >= LAG else None
    rot, site = refs[:2]
    e_out, kept, hop, swap, current, early = refs[-6:]
    x, zl = meta[0], meta[1]
    turn = tick - LAG * x
    valid = (turn >= 0) & (turn < ITEMS)
    item = item_of(tick, x)
    k, own = lax.rem(item, 4), item // 4
    sec = 2 * zl + own
    target = meta[2 + 4 * k + sec]

    if tick == 0:
        e_out[...] = jnp.zeros_like(e_out)

    @pl.when(x == 0)
    def _():
        current[...] = env[item]

    if tick >= LAG:

        @pl.when(x != 0)
        def _():
            current[...] = arrived[...]

    @pl.when(valid)
    def _():
        def site_step(s, carry):
            middle = jnp.dot(current[...], rot[s, target], preferred_element_type=jnp.float32).astype(jnp.bfloat16)
            total = consts[4 * s + k] * site[s, own].astype(jnp.float32)
            for d in range(LOCAL):
                cols = slice(d * BLK, (d + 1) * BLK)
                total += lax.dot_general(rot[s, sec, :, cols], middle[:, cols], FIRST_AXES, preferred_element_type=jnp.float32)
            new = total.astype(jnp.bfloat16)
            current[...] = new
            e_out[own, s] += consts[16 + 4 * s + k] * new.astype(jnp.float32)

            @pl.when(s == 1)
            def _():
                early[...] = new

            return carry

        lax.fori_loop(0, 4, site_step, 0)
        hop[...] = current[...]

        @pl.when(zl == 0)
        def _():
            kept[item] = early[...]
            swap[tick % 2] = current[...]

        @pl.when(zl == 1)
        def _():
            kept[item] = current[...]
            swap[tick % 2] = early[...]


def step(tick, meta, consts, env, arrived, rot, site, energy, kept, pair):
    vmem, smem = pl.BlockSpec(memory_space=pltpu.VMEM), pl.BlockSpec(memory_space=pltpu.SMEM)
    operands = [env]
    if tick >= LAG:
        operands.append(arrived)
    operands += [rot, site]
    aliases = {}
    if tick > 0:
        aliases = {2 + len(operands): 0, 3 + len(operands): 1}
        operands += [energy, kept]
    if tick % 2 == 1:
        aliases[2 + len(operands)] = 3
        operands.append(pair)
    return pl.pallas_call(
        functools.partial(step_kernel, tick),
        in_specs=[smem, smem] + [vmem] * len(operands),
        out_specs=(vmem,) * 4,
        out_shape=(
            pltpu.VMEM((2, 4, BLK, BLK), jnp.float32),
            pltpu.VMEM((ITEMS, BLK, BLK), jnp.bfloat16),
            pltpu.VMEM((BLK, BLK), jnp.bfloat16),
            pltpu.VMEM((2, BLK, BLK), jnp.bfloat16),
        ),
        scratch_shapes=[pltpu.VMEM((BLK, BLK), jnp.bfloat16)] * 2,
        input_output_aliases=aliases,
        compiler_params=pltpu.CompilerParams(vmem_limit_bytes=STEP_LIMIT),
        cost_estimate=pl.CostEstimate(flops=4 * 4 * BLK * BLK * WIDE, bytes_accessed=1 << 20, transcendentals=0),
        name="renormalize",
    )(meta, consts, *[held(v) for v in operands])


def finish_kernel(meta, kept, *refs):
    pairs, out, sem = refs[:-2], refs[-2], refs[-1]
    x, zl = meta[0], meta[1]
    copies = []
    for item in range(ITEMS):
        copies.append((None, pltpu.make_async_copy(kept.at[item], out.at[item % 4, 2 * zl + item // 4], sem.at[item])))
    for n, ref in enumerate(pairs):
        for i in range(2):
            item = 2 * n + i - LAG * x
            known = (item >= 0) & (item < ITEMS)
            past = jnp.clip(item, 0, ITEMS - 1)
            to = out.at[lax.rem(past, 4), 2 * (1 - zl) + past // 4]
            copies.append((known, pltpu.make_async_copy(ref.at[i], to, sem.at[ITEMS + 2 * n + i])))
    for known, copy in copies:
        if known is None:
            copy.start()
        else:
            pl.when(known)(copy.start)
    for known, copy in copies:
        if known is None:
            copy.wait()
        else:
            pl.when(known)(copy.wait)


def finish(meta, kept, pairs):
    vmem = pl.BlockSpec(memory_space=pltpu.VMEM)
    return pl.pallas_call(
        finish_kernel,
        in_specs=[pl.BlockSpec(memory_space=pltpu.SMEM)] + [vmem] * (1 + len(pairs)),
        out_specs=pl.BlockSpec(memory_space=pl.ANY),
        out_shape=jax.ShapeDtypeStruct((4, SECT, BLK, BLK), jnp.bfloat16),
        scratch_shapes=[pltpu.SemaphoreType.DMA((ITEMS + 2 * len(pairs),))],
        compiler_params=pltpu.CompilerParams(vmem_limit_bytes=STEP_LIMIT),
        name="finish",
    )(meta, kept, *pairs)


def piece(value, axis, place, size):
    return lax.dynamic_slice_in_dim(value, place * size, size, axis)


def on_core(body, place, operands, shapes, out_hbm=False):
    vmem = pl.BlockSpec(memory_space=pltpu.VMEM)
    return pl.pallas_call(
        body,
        in_specs=[pl.BlockSpec(memory_space=pltpu.SMEM)] + [vmem] * len(operands),
        out_specs=(vmem,) * len(shapes),
        out_shape=tuple(jax.ShapeDtypeStruct(shape, dtype) for shape, dtype in shapes),
        compiler_params=pltpu.CompilerParams(vmem_limit_bytes=2 * STEP_LIMIT),
        name=body.__name__,
    )(place, *operands)


HALF, QUARTER = BLK // 2, BLK // 8
AROUND = (1, -1, 2)


def rows_of(place, count):
    return pl.ds(pl.multiple_of(place * count, count), count)


def halve(place, energy, out):
    out[...] = energy[:, :, rows_of(1 - place[2], HALF), :].astype(jnp.bfloat16)


def quarter(place, energy, got, own, *outs):
    own_rows, y = rows_of(place[2], HALF), place[1]

    def total(at):
        first = pl.multiple_of(place[2] * HALF + at * QUARTER, QUARTER)
        return energy[:, :, pl.ds(first, QUARTER), :] + got[:, :, rows_of(at, QUARTER), :].astype(jnp.float32)

    own[...] = total(y)
    for out, step in zip(outs, AROUND):
        out[...] = total(lax.rem(y + NY + step, NY)).astype(jnp.bfloat16)


def by_site(place, own, first, second, third, mine, *outs):
    zh = place[0] // 2

    def total(at):
        return own[:, at] + (first[:, at].astype(jnp.float32) + second[:, at].astype(jnp.float32) + third[:, at].astype(jnp.float32))

    mine[...] = total(zh)
    for out, step in zip(outs, AROUND):
        out[...] = total(lax.rem(zh + NZH + step, NZH)).astype(jnp.bfloat16)


def add_up(place, mine, first, second, third, out):
    total = mine[...] + (first[...].astype(jnp.float32) + second[...].astype(jnp.float32) + third[...].astype(jnp.float32))
    out[...] = total.astype(jnp.bfloat16)


def line_up(place, *refs):
    out, zh = refs[4], place[0] // 2
    for r in range(4):
        origin = lax.rem(zh - r + 4, 4)
        out[lax.rem(origin, 2), pl.ds(2 * (origin // 2), 2)] = refs[r][...]


def join_y(place, own, first, second, third, out):
    out[:, :, rows_of(place[1], QUARTER), :] = own[...]
    for ref, step in zip((first, second, third), AROUND):
        out[:, :, rows_of(lax.rem(place[1] + NY - step, NY), QUARTER), :] = ref[...]


def join_core(place, own, other, out):
    out[:, :, rows_of(place[2], HALF), :] = own[...].astype(jnp.float32)
    out[:, :, rows_of(1 - place[2], HALF), :] = other[...].astype(jnp.float32)


def reduce_energy(energy, place, finished):
    bf16, f32 = jnp.bfloat16, jnp.float32
    energy = held(energy)
    (theirs,) = on_core(halve, place, [energy], [((2, 4, HALF, BLK), bf16)])
    got = other_core(theirs)
    shape = (2, 4, QUARTER, BLK)
    own, *parts = on_core(quarter, place, [energy, got], [(shape, f32)] + [(shape, bf16)] * 3)
    parts = [along_y(part, step) for part, step in zip(parts, AROUND)]
    shape = (2, QUARTER, BLK)
    mine, *parts = on_core(by_site, place, [own, *parts], [(shape, f32)] + [(shape, bf16)] * 3)
    parts = [along_z(part, 2 * step) for part, step in zip(parts, AROUND)]
    (total,) = on_core(add_up, place, [mine, *parts], [(shape, bf16)])
    parts = []
    for r in range(4):

        def rule(x, z, y, c):
            zh, zl = z // 2, z % 2
            return x, 2 * ((2 * zl + zh % 2 + r) % 4) + zh // 2, y, c

        parts.append(send(total, rule))
    (flat,) = on_core(line_up, place, parts, [((2, 4, QUARTER, BLK), bf16)])
    out, flat = lax.optimization_barrier((finished(), flat))
    parts = [along_y(flat, step) for step in AROUND]
    (flat,) = on_core(join_y, place, [flat, *parts], [((2, 4, HALF, BLK), bf16)])
    (flat,) = on_core(join_core, place, [flat, other_core(flat)], [((2, 4, BLK, BLK), f32)])
    return out[None], flat


def pick_kernel(pair_of, coupling, weight, out):
    for s in range(2):
        for k in range(4):
            out[4 * s + k] = coupling[s, pair_of[k]]
            out[8 + 4 * s + k] = weight[s, pair_of[k]]


def pick(pair_of, coupling, weight):
    smem = pl.BlockSpec(memory_space=pltpu.SMEM)
    return pl.pallas_call(
        pick_kernel,
        in_specs=[smem] * 3,
        out_specs=smem,
        out_shape=jax.ShapeDtypeStruct((16,), jnp.float32),
        name="pick",
    )(pair_of, coupling, weight)


def local(environment, rotations, site_terms, pair_of, targets, coupling, energy_coef):
    sweep, op = lax.axis_index("sweep"), lax.axis_index("op")
    x, zl = sweep // 2, sweep % 2
    zh, y, c = op // 8, (op // 2) % 4, op % 2
    z = 2 * zh + zl

    wide = jnp.concatenate([rotations, site_terms], axis=3)
    mine, theirs = wide[c], wide[1 - c]
    got = other_core(theirs)
    block = jnp.where(c == 0, jnp.concatenate([mine, got], axis=1), jnp.concatenate([got, mine], axis=1))
    place = jnp.stack([z, y, c, zl]).astype(jnp.int32)
    values = pick(pair_of, coupling, energy_coef).reshape(2, 8)
    got = other_lane(values)
    consts = jnp.where(zl == 0, jnp.concatenate([values, got], axis=1), jnp.concatenate([got, values], axis=1)).reshape(-1)
    meta = jnp.concatenate([jnp.stack([x, zl]).astype(jnp.int32), targets.reshape(-1)])
    env = piece(environment, 1, zl, 2).swapaxes(0, 1).reshape(ITEMS, BLK, BLK)
    rot, site, (consts, meta, env) = gather_plane(block, place, (consts, meta, env))

    energy, kept, pair = None, None, None
    hops, pairs = [], []
    for tick in range(TICKS):
        arrived = hops[tick - LAG] if tick >= LAG else None
        if tick >= 4 and tick % 2 == 0:
            arrived, pairs[tick // 2 - 2] = lax.optimization_barrier((arrived, pairs[tick // 2 - 2]))
        energy, kept, hop, pair = step(tick, meta, consts, env, arrived, rot, site, energy, kept, pair)
        hops.append(next_stage(hop) if tick < TICKS - LAG else None)
        if tick % 2 == 1:
            pairs.append(other_lane(pair))
    return reduce_energy(energy, place, lambda: finish(meta, kept, pairs))


def solution(mesh):
    return jax.shard_map(
        local,
        mesh=mesh,
        in_specs=(
            P("op", None, None, None),
            P("sweep", None, "op", None),
            P("sweep", None, "op", None),
            P("op"),
            P("op", None),
            P("sweep", None),
            P("sweep", None),
        ),
        out_specs=(P("sweep", "op", None, None, None), P("sweep", None, None, None)),
        check_vma=False,
    )
```

```python
import functools

import jax
import jax.numpy as jnp
from jax import lax
from jax.experimental import pallas as pl
from jax.experimental.pallas import tpu as pltpu
from jax.sharding import PartitionSpec as P

NX, NZL, NZH, NY, NC = 4, 2, 4, 4, 2
NZ = NZL * NZH
SECT, BLK, LOCAL = 4, 256, 4
WIDE = LOCAL * BLK
BOTH = WIDE + BLK
ITEMS = 8
LAG = 2
TICKS = ITEMS + LAG * (NX - 1)
STEP_LIMIT = 8 * 1024 * 1024

FIRST_AXES = (((0,), (0,)), ((), ()))
AXES = ("sweep", "op")


def number(x, z, y, c):
    zh, zl = z // 2, z % 2
    return (x * NZL + zl) * (NZH * NY * NC) + (zh * NY + y) * NC + c


def send(value, rule):
    pairs = []
    for x in range(NX):
        for z in range(NZ):
            for y in range(NY):
                for c in range(NC):
                    to = rule(x, z, y, c)
                    if to is not None:
                        pairs.append((number(x, z, y, c), number(*to)))
    return lax.ppermute(value, AXES, pairs)


def along_y(value, step):
    return send(value, lambda x, z, y, c: (x, z, (y + step) % NY, c))


def along_z(value, step):
    return send(value, lambda x, z, y, c: (x, (z + step) % NZ, y, c))


def other_core(value):
    return send(value, lambda x, z, y, c: (x, z, y, 1 - c))


def other_lane(value):
    return send(value, lambda x, z, y, c: (x, z ^ 1, y, c))


def next_stage(value):
    return send(value, lambda x, z, y, c: (x + 1, z, y, c) if x + 1 < NX else None)


def after(value, *others):
    return lax.optimization_barrier((value, others))[0]


def held(value):
    return pltpu.with_memory_space_constraint(value, pltpu.VMEM)


def put_kernel(layout, place, *refs):
    both, sem = refs[-2:]
    z, y, c = place[0], place[1], place[2]
    copies = []
    for n, (ref, (source, other, near, wide)) in enumerate(zip(refs, layout)):
        core = 1 - c if other else c
        does = None if source is None else core == source
        for lead, (p, q) in enumerate(zip(near, wide)):
            zs = lax.rem(z + NZ + jnp.where(core == 0, p[0], q[0]), NZ)
            ys = lax.rem(y + NY + jnp.where(core == 0, p[1], q[1]), NY)
            row = pl.ds(pl.multiple_of(((zs // 2) * NY + ys) * 16, 16), 16)
            to = both.at[2 * lax.rem(zs, 2) + core, :, row, :]
            copies.append((does, pltpu.make_async_copy(ref.at[lead], to, sem.at[n, lead])))
    for does, copy in copies:
        if does is None:
            copy.start()
        else:
            pl.when(does)(copy.start)
    for does, copy in copies:
        if does is None:
            copy.wait()
        else:
            pl.when(does)(copy.wait)


def put(place, pieces, into):
    layout = [where for _, where in pieces]
    values = [value for value, _ in pieces]
    count = len(pieces)
    vmem, anywhere = pl.BlockSpec(memory_space=pltpu.VMEM), pl.BlockSpec(memory_space=pl.ANY)
    extra = [] if into is None else [held(into)]
    return pl.pallas_call(
        functools.partial(put_kernel, layout),
        out_shape=pltpu.VMEM((4, SECT, BLK, BOTH), jnp.bfloat16),
        in_specs=[pl.BlockSpec(memory_space=pltpu.SMEM)] + [anywhere] * count + [vmem] * len(extra),
        out_specs=vmem,
        scratch_shapes=[pltpu.SemaphoreType.DMA((count, 4))],
        input_output_aliases={} if into is None else {1 + count: 0},
        compiler_params=pltpu.CompilerParams(vmem_limit_bytes=STEP_LIMIT),
        name="put",
    )(place, *values, *extra)


def by_core(value, near, wide):
    def rule(x, z, y, c):
        move = near if c == 0 else wide
        if move is None:
            return None
        return x, (z + move[0]) % NZ, (y + move[1]) % NY, c

    return send(value, rule)


def gather_plane(block, place, extra, prepare):
    together = lax.optimization_barrier
    up, down, right, left = (1, 0), (-1, 0), (0, 1), (0, -1)
    up2, down2, right2 = (2, 0), (-2, 0), (0, 2)
    right2, up2, down2 = (0, 2), (2, 0), (-2, 0)
    near = [by_core(block, right, up), by_core(block, left, down), by_core(block, right2, up2), by_core(block, None, down2)]
    lower, upper, lower2, upper2 = together(tuple(near))
    head = jnp.stack([block, lower, lower2, upper])

    lower3, lower4, upper3 = by_core(lower, None, up2), by_core(lower2, None, up2), by_core(upper, None, down2)
    lead, lag = by_core(head, up, right), by_core(head, down, left)
    lead, lag, lower3, lower4, upper3 = together((lead, lag, lower3, lower4, upper3))
    third, fourth = choose(place, [lead, lag], [[lower3, lower4, upper2, upper3]] * 2)

    lead2, lag2 = by_core(third, up, right), by_core(fourth, down, left)
    lead2, lag2, head, lead, lag = together((lead2, lag2, head, lead, lag))
    up_halves, down_halves = choose(place, [lead2, lag2], [lead, lag2], True)
    up_halves, down_halves, extra = together((up_halves, down_halves, extra))
    extra = prepare(extra)

    lead3 = [by_core(half, up, right) for half in up_halves]
    lag3 = [by_core(half, down, left) for half in down_halves]
    ready = [(head, HEAD), (lead, LEAD), (lag, LAG1)]
    ready += [(other_core(v), from_other(w)) for v, w in ready]
    ready += [(third, TAIL), (core_to_core(third, 1), from_other(TAIL))]
    lead3, lag3, extra = together((lead3, lag3, extra))

    far = by_core(lead3[0], up, None), by_core(lag3[1], down, None)
    into = put(place, ready, None)
    ready = [(lead2, LEAD2), (lag2, LAG2)]
    into = put(place, ready + [(other_core(v), from_other(w)) for v, w in ready], into)
    ready = [(v, w) for v, w in zip([*lead3, *lag3], LEAD3 + LAG3)]
    ready += [(other_core(v), from_other(w)) for v, w in ready]
    far, into = together((far, into))
    for v, w in zip(far, FAR):
        ready += [(v, w), (core_to_core(v, 0), from_other(w))]
    return put(place, ready, into), extra


def choose_kernel(parts, place, *refs):
    values, outs = refs[:-parts], refs[-parts:]
    half = parts // 2
    rest = (len(values) - 2) // 2

    def fill(n, sources):
        for m in range(4):
            out = outs[n * half + (m // 2 if half == 2 else 0)]
            at = m % 2 if half == 2 else m
            out[at] = sources[0][m] if len(sources) == 1 else sources[m][...]

    for n in range(2):
        pl.when(place[2] == 0)(functools.partial(fill, n, values[n : n + 1]))
        pl.when(place[2] == 1)(functools.partial(fill, n, values[2 + n * rest : 2 + (n + 1) * rest]))


def choose(place, zero, one, in_two=False):
    one = [v if isinstance(v, list) else [v] for v in one]
    values = [*zero, *one[0], *one[1]]
    parts = 4 if in_two else 2
    shape = (2 if in_two else 4, *zero[0].shape[1:])
    vmem = pl.BlockSpec(memory_space=pltpu.VMEM)
    outs = pl.pallas_call(
        functools.partial(choose_kernel, parts),
        in_specs=[pl.BlockSpec(memory_space=pltpu.SMEM)] + [vmem] * len(values),
        out_specs=(vmem,) * parts,
        out_shape=(jax.ShapeDtypeStruct(shape, zero[0].dtype),) * parts,
        compiler_params=pltpu.CompilerParams(vmem_limit_bytes=STEP_LIMIT),
        name="choose",
    )(place, *values)
    return (outs[:2], outs[2:]) if in_two else outs


def core_to_core(value, source):
    return send(value, lambda x, z, y, c: (x, z, y, 1 - c) if c == source else None)


def rows_at(dz):
    return [(dz, dy) for dy in (0, -1, 2, 1)]


def column_at(dy, zs):
    return [(dz, dy) for dz in zs]


def in_halves(source, near, wide):
    return tuple((source, False, near[n : n + 2], wide[n : n + 2]) for n in (0, 2))


def from_other(where):
    return (where[0], True, *where[2:])


Z_HEAD, Z_TAIL = (0, -1, -2, 1), (-3, 4, 2, 3)
HEAD = (None, False, rows_at(0), column_at(0, Z_HEAD))
LEAD = (None, False, rows_at(-1), column_at(-1, Z_HEAD))
LAG1 = (None, False, rows_at(1), column_at(1, Z_HEAD))
TAIL = (1, False, column_at(0, Z_TAIL), column_at(0, Z_TAIL))
LEAD2 = (None, False, rows_at(-2), column_at(-1, Z_TAIL))
LAG2 = (None, False, rows_at(2), column_at(1, Z_TAIL))
LEAD3 = in_halves(None, rows_at(-3), column_at(2, Z_HEAD))
LAG3 = in_halves(None, rows_at(3), column_at(2, Z_TAIL))
FAR = in_halves(0, rows_at(4), rows_at(4))


def item_of(tick, x):
    return jnp.clip(tick - LAG * x, 0, ITEMS - 1)


def step_kernel(tick, which, meta, consts, env, *refs):
    refs = list(refs)
    arrived = refs.pop(0) if tick >= LAG else None
    both = refs[0]
    e_out, kept, hop, *swaps, current, early = refs[-5 - len(which) :]
    x, zl = meta[0], meta[1]
    turn = tick - LAG * x
    valid = (turn >= 0) & (turn < ITEMS)
    item = item_of(tick, x)
    k, own = lax.rem(item, 4), item // 4
    sec = 2 * zl + own
    target = meta[2 + 4 * k + sec]

    if tick == 0:
        e_out[...] = jnp.zeros_like(e_out)

    @pl.when(x == 0)
    def _():
        current[...] = env[item]

    if tick >= LAG:

        @pl.when(x != 0)
        def _():
            current[...] = arrived[...]

    @pl.when(valid)
    def _():
        def site_step(s, carry):
            middle = jnp.dot(current[...], both[s, target, :, :WIDE], preferred_element_type=jnp.float32).astype(jnp.bfloat16)
            total = consts[4 * s + k] * both[s, sec, :, WIDE:].astype(jnp.float32)
            for d in range(LOCAL):
                cols = slice(d * BLK, (d + 1) * BLK)
                total += lax.dot_general(both[s, sec, :, cols], middle[:, cols], FIRST_AXES, preferred_element_type=jnp.float32)
            new = total.astype(jnp.bfloat16)
            current[...] = new
            e_out[own, s] += consts[16 + 4 * s + k] * new.astype(jnp.float32)

            @pl.when(s == 1)
            def _():
                early[...] = new

            return carry

        lax.fori_loop(0, 4, site_step, 0)
        hop[...] = current[...]

        @pl.when(zl == 0)
        def _():
            kept[item] = early[...]

        @pl.when(zl == 1)
        def _():
            kept[item] = current[...]

        for half, swap in zip(which, swaps):

            @pl.when((own == half) & (zl == 0))
            def _():
                swap[k] = current[...]

            @pl.when((own == half) & (zl == 1))
            def _():
                swap[k] = early[...]


def halves_at(tick):
    turns = [tick - LAG * x for x in range(NX)]
    return [half for half in range(2) if any(4 * half <= turn < 4 * half + 4 for turn in turns)]


def step(tick, meta, consts, env, arrived, both, energy, kept, swaps):
    vmem, smem = pl.BlockSpec(memory_space=pltpu.VMEM), pl.BlockSpec(memory_space=pltpu.SMEM)
    which = halves_at(tick)
    operands = [env]
    if tick >= LAG:
        operands.append(arrived)
    operands += [both]
    aliases = {}
    if tick > 0:
        aliases = {2 + len(operands): 0, 3 + len(operands): 1}
        operands += [energy, kept]
    for n, half in enumerate(which):
        if half in swaps:
            aliases[2 + len(operands)] = 3 + n
            operands.append(swaps[half])
    energy, kept, hop, *outs = pl.pallas_call(
        functools.partial(step_kernel, tick, which),
        in_specs=[smem, smem] + [vmem] * len(operands),
        out_specs=(vmem,) * (3 + len(which)),
        out_shape=(
            pltpu.VMEM((2, 4, BLK, BLK), jnp.float32),
            pltpu.VMEM((ITEMS, BLK, BLK), jnp.bfloat16),
            pltpu.VMEM((BLK, BLK), jnp.bfloat16),
        )
        + (pltpu.VMEM((4, BLK, BLK), jnp.bfloat16),) * len(which),
        scratch_shapes=[pltpu.VMEM((BLK, BLK), jnp.bfloat16)] * 2,
        input_output_aliases=aliases,
        compiler_params=pltpu.CompilerParams(vmem_limit_bytes=STEP_LIMIT),
        name="renormalize",
    )(meta, consts, *[held(v) for v in operands])
    return energy, kept, hop, dict(zip(which, outs))


def place_kernel(half, meta, *refs):
    other, out, sem = refs[0], refs[-2], refs[-1]
    zl = meta[1]
    copies = [pltpu.make_async_copy(other.at[k], out.at[k, 2 * (1 - zl) + half], sem.at[k]) for k in range(4)]
    if half == 0:
        kept = refs[1]
        for item in range(ITEMS):
            copies.append(pltpu.make_async_copy(kept.at[item], out.at[item % 4, 2 * zl + item // 4], sem.at[4 + item]))
    for copy in copies:
        copy.start()
    for copy in copies:
        copy.wait()


def place_items(half, meta, other, rest):
    vmem, hbm = pl.BlockSpec(memory_space=pltpu.VMEM), pl.BlockSpec(memory_space=pltpu.HBM)
    return pl.pallas_call(
        functools.partial(place_kernel, half),
        in_specs=[pl.BlockSpec(memory_space=pltpu.SMEM), vmem, vmem if half == 0 else hbm],
        out_specs=hbm,
        out_shape=pltpu.HBM((4, SECT, BLK, BLK), jnp.bfloat16),
        scratch_shapes=[pltpu.SemaphoreType.DMA((4 + ITEMS,))],
        input_output_aliases={} if half == 0 else {2: 0},
        compiler_params=pltpu.CompilerParams(vmem_limit_bytes=STEP_LIMIT),
        name="place_items",
    )(meta, other, rest)


def piece(value, axis, place, size):
    return lax.dynamic_slice_in_dim(value, place * size, size, axis)


def on_core(body, place, operands, shapes, out_hbm=False):
    vmem = pl.BlockSpec(memory_space=pltpu.VMEM)
    return pl.pallas_call(
        body,
        in_specs=[pl.BlockSpec(memory_space=pltpu.SMEM)] + [vmem] * len(operands),
        out_specs=(vmem,) * len(shapes),
        out_shape=tuple(jax.ShapeDtypeStruct(shape, dtype) for shape, dtype in shapes),
        compiler_params=pltpu.CompilerParams(vmem_limit_bytes=2 * STEP_LIMIT),
        name=body.__name__,
    )(place, *operands)


HALF, QUARTER = BLK // 2, BLK // 8
AROUND = (1, -1, 2)


def rows_of(place, count):
    return pl.ds(pl.multiple_of(place * count, count), count)


def halve(place, energy, out):
    out[...] = energy[:, :, rows_of(1 - place[2], HALF), :].astype(jnp.bfloat16)


def quarter(place, energy, got, own, *outs):
    own_rows, y = rows_of(place[2], HALF), place[1]

    def total(at):
        first = pl.multiple_of(place[2] * HALF + at * QUARTER, QUARTER)
        return energy[:, :, pl.ds(first, QUARTER), :] + got[:, :, rows_of(at, QUARTER), :].astype(jnp.float32)

    own[...] = total(y)
    for out, step in zip(outs, AROUND):
        out[...] = total(lax.rem(y + NY + step, NY)).astype(jnp.bfloat16)


def by_site(place, own, first, second, third, mine, *outs):
    zh = place[0] // 2

    def total(at):
        return own[:, at] + (first[:, at].astype(jnp.float32) + second[:, at].astype(jnp.float32) + third[:, at].astype(jnp.float32))

    mine[...] = total(zh)
    for out, step in zip(outs, AROUND):
        out[...] = total(lax.rem(zh + NZH + step, NZH)).astype(jnp.bfloat16)


def add_up(place, mine, first, second, third, out):
    total = mine[...] + (first[...].astype(jnp.float32) + second[...].astype(jnp.float32) + third[...].astype(jnp.float32))
    out[...] = total.astype(jnp.bfloat16)


def line_up(place, *refs):
    out, zh = refs[4], place[0] // 2
    for r in range(4):
        origin = lax.rem(zh - r + 4, 4)
        out[lax.rem(origin, 2), pl.ds(2 * (origin // 2), 2)] = refs[r][...]


def join_y(place, own, first, second, third, out):
    out[:, :, rows_of(place[1], QUARTER), :] = own[...]
    for ref, step in zip((first, second, third), AROUND):
        out[:, :, rows_of(lax.rem(place[1] + NY - step, NY), QUARTER), :] = ref[...]


def join_core(place, own, other, out):
    out[:, :, rows_of(place[2], HALF), :] = own[...].astype(jnp.float32)
    out[:, :, rows_of(1 - place[2], HALF), :] = other[...].astype(jnp.float32)


def reduce_energy(energy, place, meta, kept, ended):
    bf16, f32 = jnp.bfloat16, jnp.float32
    energy = held(energy)
    (theirs,) = on_core(halve, place, [energy], [((2, 4, HALF, BLK), bf16)])
    got = other_core(theirs)
    shape = (2, 4, QUARTER, BLK)
    own, *parts = on_core(quarter, place, [energy, got], [(shape, f32)] + [(shape, bf16)] * 3)
    parts = [along_y(part, step) for part, step in zip(parts, AROUND)]
    shape = (2, QUARTER, BLK)
    mine, *parts = on_core(by_site, place, [own, *parts], [(shape, f32)] + [(shape, bf16)] * 3)
    parts = [along_z(part, 2 * step) for part, step in zip(parts, AROUND)]
    (total,) = on_core(add_up, place, [mine, *parts], [(shape, bf16)])
    parts = []
    for r in range(4):

        def rule(x, z, y, c):
            zh, zl = z // 2, z % 2
            return x, 2 * ((2 * zl + zh % 2 + r) % 4) + zh // 2, y, c

        parts.append(send(total, rule))
    (flat,) = on_core(line_up, place, parts, [((2, 4, QUARTER, BLK), bf16)])
    out = place_items(0, meta, other_lane(ended[0]), kept)
    flat, late, out = lax.optimization_barrier((flat, ended[1], out))
    out = place_items(1, meta, other_lane(late), out)
    parts = [along_y(flat, step) for step in AROUND]
    (flat,) = on_core(join_y, place, [flat, *parts], [((2, 4, HALF, BLK), bf16)])
    (flat,) = on_core(join_core, place, [flat, other_core(flat)], [((2, 4, BLK, BLK), f32)])
    return out[None], flat


def pick_kernel(pair_of, coupling, weight, out):
    for s in range(2):
        for k in range(4):
            out[4 * s + k] = coupling[s, pair_of[k]]
            out[8 + 4 * s + k] = weight[s, pair_of[k]]


def pick(pair_of, coupling, weight):
    smem = pl.BlockSpec(memory_space=pltpu.SMEM)
    return pl.pallas_call(
        pick_kernel,
        in_specs=[smem] * 3,
        out_specs=smem,
        out_shape=jax.ShapeDtypeStruct((16,), jnp.float32),
        name="pick",
    )(pair_of, coupling, weight)


def local(environment, rotations, site_terms, pair_of, targets, coupling, energy_coef):
    sweep, op = lax.axis_index("sweep"), lax.axis_index("op")
    x, zl = sweep // 2, sweep % 2
    zh, y, c = op // 8, (op // 2) % 4, op % 2
    z = 2 * zh + zl

    wide = jnp.concatenate([rotations, site_terms], axis=3)
    mine, theirs = wide[c], wide[1 - c]
    got = other_core(theirs)
    block = jnp.where(c == 0, jnp.concatenate([mine, got], axis=1), jnp.concatenate([got, mine], axis=1))
    place = jnp.stack([z, y, c, zl]).astype(jnp.int32)

    def prepare(operands):
        pair_of, targets, coupling, energy_coef, environment = operands
        values = pick(pair_of, coupling, energy_coef).reshape(2, 8)
        got = other_lane(values)
        consts = jnp.where(zl == 0, jnp.concatenate([values, got], axis=1), jnp.concatenate([got, values], axis=1)).reshape(-1)
        meta = jnp.concatenate([jnp.stack([x, zl]).astype(jnp.int32), targets.reshape(-1)])
        env = piece(environment, 1, zl, 2).swapaxes(0, 1).reshape(ITEMS, BLK, BLK)
        return consts, meta, env

    operands = (pair_of, targets, coupling, energy_coef, environment)
    both, (consts, meta, env) = gather_plane(block, place, operands, prepare)

    energy, kept, swaps, hops, ended = None, None, {}, [], {}
    for tick in range(TICKS):
        arrived = hops[tick - LAG] if tick >= LAG else None
        energy, kept, hop, swaps = step(tick, meta, consts, env, arrived, both, energy, kept, swaps)
        hops.append(next_stage(hop) if tick < TICKS - LAG else None)
        for half in swaps:
            if half not in halves_at(tick + 1):
                ended[half] = swaps[half]
    return reduce_energy(energy, place, meta, kept, ended)


def solution(mesh):
    return jax.shard_map(
        local,
        mesh=mesh,
        in_specs=(
            P("op", None, None, None),
            P("sweep", None, "op", None),
            P("sweep", None, "op", None),
            P("op"),
            P("op", None),
            P("sweep", None),
            P("sweep", None),
        ),
        out_specs=(P("sweep", "op", None, None, None), P("sweep", None, None, None)),
        check_vma=False,
    )
```

```python
import functools

import jax
import jax.numpy as jnp
from jax import lax
from jax.experimental import pallas as pl
from jax.experimental.pallas import tpu as pltpu
from jax.sharding import PartitionSpec as P

NX, NZL, NZH, NY, NC = 4, 2, 4, 4, 2
NZ = NZL * NZH
SECT, BLK, LOCAL = 4, 256, 4
WIDE = LOCAL * BLK
BOTH = WIDE + BLK
ITEMS = 8
SPLIT = 4
PARTS = ((0, SPLIT), (SPLIT, ITEMS))
LAG = 2
TICKS = ITEMS + LAG * (NX - 1)
STEP_LIMIT = 8 * 1024 * 1024

FIRST_AXES = (((0,), (0,)), ((), ()))
AXES = ("sweep", "op")


def number(x, z, y, c):
    zh, zl = z // 2, z % 2
    return (x * NZL + zl) * (NZH * NY * NC) + (zh * NY + y) * NC + c


def send(value, rule):
    pairs = []
    for x in range(NX):
        for z in range(NZ):
            for y in range(NY):
                for c in range(NC):
                    to = rule(x, z, y, c)
                    if to is not None:
                        pairs.append((number(x, z, y, c), number(*to)))
    return lax.ppermute(value, AXES, pairs)


def along_y(value, step):
    return send(value, lambda x, z, y, c: (x, z, (y + step) % NY, c))


def along_z(value, step):
    return send(value, lambda x, z, y, c: (x, (z + step) % NZ, y, c))


def other_core(value):
    return send(value, lambda x, z, y, c: (x, z, y, 1 - c))


def other_lane(value):
    return send(value, lambda x, z, y, c: (x, z ^ 1, y, c))


def next_stage(value):
    return send(value, lambda x, z, y, c: (x + 1, z, y, c) if x + 1 < NX else None)


def after(value, *others):
    return lax.optimization_barrier((value, others))[0]


def held(value):
    return pltpu.with_memory_space_constraint(value, pltpu.VMEM)


def put_kernel(layout, place, *refs):
    both, sem = refs[-2:]
    z, y, c = place[0], place[1], place[2]
    copies = []
    for n, (ref, (source, other, near, wide)) in enumerate(zip(refs, layout)):
        core = 1 - c if other else c
        does = None if source is None else core == source
        for lead, (p, q) in enumerate(zip(near, wide)):
            zs = lax.rem(z + NZ + jnp.where(core == 0, p[0], q[0]), NZ)
            ys = lax.rem(y + NY + jnp.where(core == 0, p[1], q[1]), NY)
            row = pl.ds(pl.multiple_of(((zs // 2) * NY + ys) * 16, 16), 16)
            to = both.at[2 * lax.rem(zs, 2) + core, :, row, :]
            copies.append((does, pltpu.make_async_copy(ref.at[lead], to, sem.at[n, lead])))
    for does, copy in copies:
        if does is None:
            copy.start()
        else:
            pl.when(does)(copy.start)
    for does, copy in copies:
        if does is None:
            copy.wait()
        else:
            pl.when(does)(copy.wait)


def put(place, pieces, into):
    layout = [where for _, where in pieces]
    values = [value for value, _ in pieces]
    count = len(pieces)
    vmem, anywhere = pl.BlockSpec(memory_space=pltpu.VMEM), pl.BlockSpec(memory_space=pl.ANY)
    extra = [] if into is None else [held(into)]
    return pl.pallas_call(
        functools.partial(put_kernel, layout),
        out_shape=pltpu.VMEM((4, SECT, BLK, BOTH), jnp.bfloat16),
        in_specs=[pl.BlockSpec(memory_space=pltpu.SMEM)] + [anywhere] * count + [vmem] * len(extra),
        out_specs=vmem,
        scratch_shapes=[pltpu.SemaphoreType.DMA((count, 4))],
        input_output_aliases={} if into is None else {1 + count: 0},
        compiler_params=pltpu.CompilerParams(vmem_limit_bytes=STEP_LIMIT),
        name="put",
    )(place, *values, *extra)


def by_core(value, near, wide):
    def rule(x, z, y, c):
        move = near if c == 0 else wide
        if move is None:
            return None
        return x, (z + move[0]) % NZ, (y + move[1]) % NY, c

    return send(value, rule)


def gather_plane(block, place, extra, prepare):
    together = lax.optimization_barrier
    up, down, right, left = (1, 0), (-1, 0), (0, 1), (0, -1)
    up2, down2, right2 = (2, 0), (-2, 0), (0, 2)
    right2, up2, down2 = (0, 2), (2, 0), (-2, 0)
    near = [by_core(block, right, up), by_core(block, left, down), by_core(block, right2, up2), by_core(block, None, down2)]
    lower, upper, lower2, upper2 = together(tuple(near))
    head = jnp.stack([block, lower, lower2, upper])

    lower3, lower4, upper3 = by_core(lower, None, up2), by_core(lower2, None, up2), by_core(upper, None, down2)
    lead, lag = by_core(head, up, right), by_core(head, down, left)
    lead, lag, lower3, lower4, upper3 = together((lead, lag, lower3, lower4, upper3))
    third, fourth = choose(place, [lead, lag], [[lower3, lower4, upper2, upper3]] * 2)
    third, fourth, extra, head, lead, lag = together((third, fourth, extra, head, lead, lag))

    lead2, lag2 = by_core(third, up, right), by_core(fourth, down, left)
    extra = prepare(extra)
    ready = [(head, HEAD), (lead, LEAD), (lag, LAG1)]
    ready += [(other_core(v), from_other(w)) for v, w in ready]
    ready += [(third, TAIL), (core_to_core(third, 1), from_other(TAIL))]
    lead2, lag2, extra = together((lead2, lag2, extra))
    up_halves, down_halves = choose(place, [lead2, lag2], [lead, lag2], True)

    lead3 = [by_core(half, up, right) for half in up_halves]
    lag3 = [by_core(half, down, left) for half in down_halves]
    into = put(place, ready, None)
    lead3, lag3, lead2, lag2, into = together((lead3, lag3, lead2, lag2, into))

    far = by_core(lead3[0], up, None), by_core(lag3[1], down, None)
    ready = [(lead2, LEAD2), (lag2, LAG2)]
    into = put(place, ready + [(other_core(v), from_other(w)) for v, w in ready], into)
    ready = [(v, w) for v, w in zip([*lead3, *lag3], LEAD3 + LAG3)]
    ready += [(other_core(v), from_other(w)) for v, w in ready]
    far, into = together((far, into))
    for v, w in zip(far, FAR):
        ready += [(v, w), (core_to_core(v, 0), from_other(w))]
    return put(place, ready, into), extra


def choose_kernel(parts, place, *refs):
    values, outs = refs[:-parts], refs[-parts:]
    half = parts // 2
    rest = (len(values) - 2) // 2

    def fill(n, sources):
        for m in range(4):
            out = outs[n * half + (m // 2 if half == 2 else 0)]
            at = m % 2 if half == 2 else m
            out[at] = sources[0][m] if len(sources) == 1 else sources[m][...]

    for n in range(2):
        pl.when(place[2] == 0)(functools.partial(fill, n, values[n : n + 1]))
        pl.when(place[2] == 1)(functools.partial(fill, n, values[2 + n * rest : 2 + (n + 1) * rest]))


def choose(place, zero, one, in_two=False):
    one = [v if isinstance(v, list) else [v] for v in one]
    values = [*zero, *one[0], *one[1]]
    parts = 4 if in_two else 2
    shape = (2 if in_two else 4, *zero[0].shape[1:])
    vmem = pl.BlockSpec(memory_space=pltpu.VMEM)
    outs = pl.pallas_call(
        functools.partial(choose_kernel, parts),
        in_specs=[pl.BlockSpec(memory_space=pltpu.SMEM)] + [vmem] * len(values),
        out_specs=(vmem,) * parts,
        out_shape=(jax.ShapeDtypeStruct(shape, zero[0].dtype),) * parts,
        compiler_params=pltpu.CompilerParams(vmem_limit_bytes=STEP_LIMIT),
        name="choose",
    )(place, *values)
    return (outs[:2], outs[2:]) if in_two else outs


def core_to_core(value, source):
    return send(value, lambda x, z, y, c: (x, z, y, 1 - c) if c == source else None)


def rows_at(dz):
    return [(dz, dy) for dy in (0, -1, 2, 1)]


def column_at(dy, zs):
    return [(dz, dy) for dz in zs]


def in_halves(source, near, wide):
    return tuple((source, False, near[n : n + 2], wide[n : n + 2]) for n in (0, 2))


def from_other(where):
    return (where[0], True, *where[2:])


Z_HEAD, Z_TAIL = (0, -1, -2, 1), (-3, 4, 2, 3)
HEAD = (None, False, rows_at(0), column_at(0, Z_HEAD))
LEAD = (None, False, rows_at(-1), column_at(-1, Z_HEAD))
LAG1 = (None, False, rows_at(1), column_at(1, Z_HEAD))
TAIL = (1, False, column_at(0, Z_TAIL), column_at(0, Z_TAIL))
LEAD2 = (None, False, rows_at(-2), column_at(-1, Z_TAIL))
LAG2 = (None, False, rows_at(2), column_at(1, Z_TAIL))
LEAD3 = in_halves(None, rows_at(-3), column_at(2, Z_HEAD))
LAG3 = in_halves(None, rows_at(3), column_at(2, Z_TAIL))
FAR = in_halves(0, rows_at(4), rows_at(4))


def item_of(tick, x):
    return jnp.clip(tick - LAG * x, 0, ITEMS - 1)


def step_kernel(tick, which, meta, consts, env, *refs):
    refs = list(refs)
    arrived = refs.pop(0) if tick >= LAG else None
    both = refs[0]
    e_out, kept, hop, *swaps, current, early = refs[-5 - len(which) :]
    x, zl = meta[0], meta[1]
    turn = tick - LAG * x
    valid = (turn >= 0) & (turn < ITEMS)
    item = item_of(tick, x)
    k, own = lax.rem(item, 4), item // 4
    sec = 2 * zl + own
    target = meta[2 + 4 * k + sec]

    if tick == 0:
        e_out[...] = jnp.zeros_like(e_out)

    @pl.when(x == 0)
    def _():
        current[...] = env[item]

    if tick >= LAG:

        @pl.when(x != 0)
        def _():
            current[...] = arrived[...]

    @pl.when(valid)
    def _():
        def two_sites(pair, carry):
            for s in (2 * pair, 2 * pair + 1):
                middle = jnp.dot(current[...], both[s, target, :, :WIDE], preferred_element_type=jnp.float32).astype(jnp.bfloat16)
                total = consts[4 * s + k] * both[s, sec, :, WIDE:].astype(jnp.float32)
                for d in range(LOCAL):
                    cols = slice(d * BLK, (d + 1) * BLK)
                    total += lax.dot_general(both[s, sec, :, cols], middle[:, cols], FIRST_AXES, preferred_element_type=jnp.float32)
                new = total.astype(jnp.bfloat16)
                current[...] = new
                e_out[own, s] += consts[16 + 4 * s + k] * new.astype(jnp.float32)

            @pl.when(pair == 0)
            def _():
                early[...] = current[...]

            return carry

        lax.fori_loop(0, 2, two_sites, 0)
        hop[...] = current[...]

        @pl.when(zl == 0)
        def _():
            kept[item] = early[...]

        @pl.when(zl == 1)
        def _():
            kept[item] = current[...]

        for part, swap in zip(which, swaps):
            first, end = PARTS[part]
            inside = (item >= first) & (item < end)

            @pl.when(inside & (zl == 0))
            def _():
                swap[item - first] = current[...]

            @pl.when(inside & (zl == 1))
            def _():
                swap[item - first] = early[...]


def parts_at(tick):
    turns = [tick - LAG * x for x in range(NX)]
    return [n for n, (first, end) in enumerate(PARTS) if any(first <= turn < end for turn in turns)]


def step(tick, meta, consts, env, arrived, both, energy, kept, swaps):
    vmem, smem = pl.BlockSpec(memory_space=pltpu.VMEM), pl.BlockSpec(memory_space=pltpu.SMEM)
    which = parts_at(tick)
    operands = [env]
    if tick >= LAG:
        operands.append(arrived)
    operands += [both]
    aliases = {}
    if tick > 0:
        aliases = {2 + len(operands): 0, 3 + len(operands): 1}
        operands += [energy, kept]
    for n, part in enumerate(which):
        if part in swaps:
            aliases[2 + len(operands)] = 3 + n
            operands.append(swaps[part])
    energy, kept, hop, *outs = pl.pallas_call(
        functools.partial(step_kernel, tick, which),
        in_specs=[smem, smem] + [vmem] * len(operands),
        out_specs=(vmem,) * (3 + len(which)),
        out_shape=(
            pltpu.VMEM((2, 4, BLK, BLK), jnp.float32),
            pltpu.VMEM((ITEMS, BLK, BLK), jnp.bfloat16),
            pltpu.VMEM((BLK, BLK), jnp.bfloat16),
        )
        + tuple(pltpu.VMEM((PARTS[n][1] - PARTS[n][0], BLK, BLK), jnp.bfloat16) for n in which),
        scratch_shapes=[pltpu.VMEM((BLK, BLK), jnp.bfloat16)] * 2,
        input_output_aliases=aliases,
        compiler_params=pltpu.CompilerParams(vmem_limit_bytes=STEP_LIMIT),
        name="renormalize",
    )(meta, consts, *[held(v) for v in operands])
    return energy, kept, hop, dict(zip(which, outs))


def place_kernel(part, meta, *refs):
    other, out, sem = refs[0], refs[-2], refs[-1]
    zl = meta[1]
    first, end = PARTS[part]
    copies = []
    for n, item in enumerate(range(first, end)):
        copies.append(pltpu.make_async_copy(other.at[n], out.at[item % 4, 2 * (1 - zl) + item // 4], sem.at[n]))
    if part == 0:
        kept = refs[1]
        for item in range(ITEMS):
            copies.append(pltpu.make_async_copy(kept.at[item], out.at[item % 4, 2 * zl + item // 4], sem.at[ITEMS + item]))
    for copy in copies:
        copy.start()
    for copy in copies:
        copy.wait()


def place_items(part, meta, other, rest):
    vmem, hbm = pl.BlockSpec(memory_space=pltpu.VMEM), pl.BlockSpec(memory_space=pltpu.HBM)
    return pl.pallas_call(
        functools.partial(place_kernel, part),
        in_specs=[pl.BlockSpec(memory_space=pltpu.SMEM), vmem, vmem if part == 0 else hbm],
        out_specs=hbm,
        out_shape=pltpu.HBM((4, SECT, BLK, BLK), jnp.bfloat16),
        scratch_shapes=[pltpu.SemaphoreType.DMA((2 * ITEMS,))],
        input_output_aliases={} if part == 0 else {2: 0},
        compiler_params=pltpu.CompilerParams(vmem_limit_bytes=STEP_LIMIT),
        name="place_items",
    )(meta, other, rest)


def piece(value, axis, place, size):
    return lax.dynamic_slice_in_dim(value, place * size, size, axis)


def on_core(body, place, operands, shapes, out_hbm=False):
    vmem = pl.BlockSpec(memory_space=pltpu.VMEM)
    return pl.pallas_call(
        body,
        in_specs=[pl.BlockSpec(memory_space=pltpu.SMEM)] + [vmem] * len(operands),
        out_specs=(vmem,) * len(shapes),
        out_shape=tuple(jax.ShapeDtypeStruct(shape, dtype) for shape, dtype in shapes),
        compiler_params=pltpu.CompilerParams(vmem_limit_bytes=2 * STEP_LIMIT),
        name=body.__name__,
    )(place, *operands)


HALF, QUARTER = BLK // 2, BLK // 8
AROUND = (1, -1, 2)
ALONG = (1, -1, 3, -3, 2, -2, 4)


def rows_of(place, count):
    return pl.ds(pl.multiple_of(place * count, count), count)


def halve(place, energy, out):
    out[...] = energy[:, :, rows_of(1 - place[2], HALF), :].astype(jnp.bfloat16)


def quarter(place, energy, got, own, *outs):
    own_rows, y = rows_of(place[2], HALF), place[1]

    def total(at):
        first = pl.multiple_of(place[2] * HALF + at * QUARTER, QUARTER)
        return energy[:, :, pl.ds(first, QUARTER), :] + got[:, :, rows_of(at, QUARTER), :].astype(jnp.float32)

    own[...] = total(y)
    for out, step in zip(outs, AROUND):
        out[...] = total(lax.rem(y + NY + step, NY)).astype(jnp.bfloat16)


def by_lane(place, own, first, second, third, mine, near, far):
    zl = place[3]

    def total(lane):
        at = pl.ds(2 * lane, 2)
        return own[:, at] + (first[:, at].astype(jnp.float32) + second[:, at].astype(jnp.float32) + third[:, at].astype(jnp.float32))

    mine[...] = total(zl)
    near[...] = mine[...].astype(jnp.bfloat16)
    far[...] = total(1 - zl).astype(jnp.bfloat16)


def line_up(place, mine, *refs):
    out, zl = refs[-1], place[3]

    def total(parity):
        return sum(ref[...].astype(jnp.float32) for ref, step in zip(refs, ALONG) if step % 2 == parity)

    same, other = mine[...] + total(0), total(1)
    for n in range(2):
        for sector in range(2):
            out[n, 2 * zl + sector] = same[sector, n].astype(jnp.bfloat16)
            out[n, 2 * (1 - zl) + sector] = other[sector, n].astype(jnp.bfloat16)


def join_y(place, own, first, second, third, out):
    out[:, :, rows_of(place[1], QUARTER), :] = own[...]
    for ref, step in zip((first, second, third), AROUND):
        out[:, :, rows_of(lax.rem(place[1] + NY - step, NY), QUARTER), :] = ref[...]


def join_core(place, own, other, out):
    out[:, :, rows_of(place[2], HALF), :] = own[...].astype(jnp.float32)
    out[:, :, rows_of(1 - place[2], HALF), :] = other[...].astype(jnp.float32)


def reduce_energy(energy, place, meta, kept, ended):
    bf16, f32 = jnp.bfloat16, jnp.float32
    energy = held(energy)
    (theirs,) = on_core(halve, place, [energy], [((2, 4, HALF, BLK), bf16)])
    got = other_core(theirs)
    shape = (2, 4, QUARTER, BLK)
    own, *parts = on_core(quarter, place, [energy, got], [(shape, f32)] + [(shape, bf16)] * 3)
    parts = [along_y(part, step) for part, step in zip(parts, AROUND)]
    shape = (2, 2, QUARTER, BLK)
    mine, near, far = on_core(by_lane, place, [own, *parts], [(shape, f32)] + [(shape, bf16)] * 2)
    parts = [along_z(far if step % 2 else near, step) for step in ALONG]
    out = place_items(0, meta, other_lane(ended[0]), kept)
    parts[-1], late, out = lax.optimization_barrier((parts[-1], ended[1], out))
    late = other_lane(late)
    (flat,) = on_core(line_up, place, [mine, *parts], [((2, 4, QUARTER, BLK), bf16)])
    out = place_items(1, meta, late, out)
    parts = [along_y(flat, step) for step in AROUND]
    (flat,) = on_core(join_y, place, [flat, *parts], [((2, 4, HALF, BLK), bf16)])
    (flat,) = on_core(join_core, place, [flat, other_core(flat)], [((2, 4, BLK, BLK), f32)])
    return out[None], flat


def pick_kernel(pair_of, coupling, weight, out):
    for s in range(2):
        for k in range(4):
            out[4 * s + k] = coupling[s, pair_of[k]]
            out[8 + 4 * s + k] = weight[s, pair_of[k]]


def pick(pair_of, coupling, weight):
    smem = pl.BlockSpec(memory_space=pltpu.SMEM)
    return pl.pallas_call(
        pick_kernel,
        in_specs=[smem] * 3,
        out_specs=smem,
        out_shape=jax.ShapeDtypeStruct((16,), jnp.float32),
        name="pick",
    )(pair_of, coupling, weight)


def local(environment, rotations, site_terms, pair_of, targets, coupling, energy_coef):
    sweep, op = lax.axis_index("sweep"), lax.axis_index("op")
    x, zl = sweep // 2, sweep % 2
    zh, y, c = op // 8, (op // 2) % 4, op % 2
    z = 2 * zh + zl

    wide = jnp.concatenate([rotations, site_terms], axis=3)
    mine, theirs = wide[c], wide[1 - c]
    got = other_core(theirs)
    block = jnp.where(c == 0, jnp.concatenate([mine, got], axis=1), jnp.concatenate([got, mine], axis=1))
    place = jnp.stack([z, y, c, zl]).astype(jnp.int32)

    def prepare(operands):
        pair_of, targets, coupling, energy_coef, environment = operands
        values = pick(pair_of, coupling, energy_coef).reshape(2, 8)
        got = other_lane(values)
        consts = jnp.where(zl == 0, jnp.concatenate([values, got], axis=1), jnp.concatenate([got, values], axis=1)).reshape(-1)
        meta = jnp.concatenate([jnp.stack([x, zl]).astype(jnp.int32), targets.reshape(-1)])
        env = piece(environment, 1, zl, 2).swapaxes(0, 1).reshape(ITEMS, BLK, BLK)
        return consts, meta, env

    operands = (pair_of, targets, coupling, energy_coef, environment)
    both, (consts, meta, env) = gather_plane(block, place, operands, prepare)

    energy, kept, swaps, hops, ended = None, None, {}, [], {}
    for tick in range(TICKS):
        arrived = hops[tick - LAG] if tick >= LAG else None
        energy, kept, hop, swaps = step(tick, meta, consts, env, arrived, both, energy, kept, swaps)
        hops.append(next_stage(hop) if tick < TICKS - LAG else None)
        for part in swaps:
            if part not in parts_at(tick + 1):
                ended[part] = swaps[part]
    return reduce_energy(energy, place, meta, kept, ended)


def solution(mesh):
    return jax.shard_map(
        local,
        mesh=mesh,
        in_specs=(
            P("op", None, None, None),
            P("sweep", None, "op", None),
            P("sweep", None, "op", None),
            P("op"),
            P("op", None),
            P("sweep", None),
            P("sweep", None),
        ),
        out_specs=(P("sweep", "op", None, None, None), P("sweep", None, None, None)),
        check_vma=False,
    )
```

```python
import functools

import jax
import jax.numpy as jnp
from jax import lax
from jax.experimental import pallas as pl
from jax.experimental.pallas import tpu as pltpu
from jax.sharding import PartitionSpec as P

NX, NZL, NZH, NY, NC = 4, 2, 4, 4, 2
NZ = NZL * NZH
SECT, BLK, LOCAL = 4, 256, 4
WIDE = LOCAL * BLK
BOTH = WIDE + BLK
ITEMS = 8
SPLIT = 4
PARTS = ((0, SPLIT), (SPLIT, ITEMS))
LAG = 2
TICKS = ITEMS + LAG * (NX - 1)
STEP_LIMIT = 8 * 1024 * 1024

FIRST_AXES = (((0,), (0,)), ((), ()))
AXES = ("sweep", "op")


def number(x, z, y, c):
    zh, zl = z // 2, z % 2
    return (x * NZL + zl) * (NZH * NY * NC) + (zh * NY + y) * NC + c


def send(value, rule):
    pairs = []
    for x in range(NX):
        for z in range(NZ):
            for y in range(NY):
                for c in range(NC):
                    to = rule(x, z, y, c)
                    if to is not None:
                        pairs.append((number(x, z, y, c), number(*to)))
    return lax.ppermute(value, AXES, pairs)


def along_y(value, step):
    return send(value, lambda x, z, y, c: (x, z, (y + step) % NY, c))


def along_z(value, step):
    return send(value, lambda x, z, y, c: (x, (z + step) % NZ, y, c))


def other_core(value):
    return send(value, lambda x, z, y, c: (x, z, y, 1 - c))


def other_lane(value):
    return send(value, lambda x, z, y, c: (x, z ^ 1, y, c))


def next_stage(value):
    return send(value, lambda x, z, y, c: (x + 1, z, y, c) if x + 1 < NX else None)


def after(value, *others):
    return lax.optimization_barrier((value, others))[0]


def held(value):
    return pltpu.with_memory_space_constraint(value, pltpu.VMEM)


def put_kernel(layout, place, *refs):
    both, sem = refs[-2:]
    z, y, c = place[0], place[1], place[2]
    copies = []
    for n, (ref, (source, other, near, wide)) in enumerate(zip(refs, layout)):
        core = 1 - c if other else c
        does = None if source is None else core == source
        for lead, (p, q) in enumerate(zip(near, wide)):
            zs = lax.rem(z + NZ + jnp.where(core == 0, p[0], q[0]), NZ)
            ys = lax.rem(y + NY + jnp.where(core == 0, p[1], q[1]), NY)
            row = pl.ds(pl.multiple_of(((zs // 2) * NY + ys) * 16, 16), 16)
            to = both.at[2 * lax.rem(zs, 2) + core, :, row, :]
            copies.append((does, pltpu.make_async_copy(ref.at[lead], to, sem.at[n, lead])))
    for does, copy in copies:
        if does is None:
            copy.start()
        else:
            pl.when(does)(copy.start)
    for does, copy in copies:
        if does is None:
            copy.wait()
        else:
            pl.when(does)(copy.wait)


def put(place, pieces, into):
    layout = [where for _, where in pieces]
    values = [value for value, _ in pieces]
    count = len(pieces)
    vmem, anywhere = pl.BlockSpec(memory_space=pltpu.VMEM), pl.BlockSpec(memory_space=pl.ANY)
    extra = [] if into is None else [held(into)]
    return pl.pallas_call(
        functools.partial(put_kernel, layout),
        out_shape=pltpu.VMEM((4, SECT, BLK, BOTH), jnp.bfloat16),
        in_specs=[pl.BlockSpec(memory_space=pltpu.SMEM)] + [anywhere] * count + [vmem] * len(extra),
        out_specs=vmem,
        scratch_shapes=[pltpu.SemaphoreType.DMA((count, 4))],
        input_output_aliases={} if into is None else {1 + count: 0},
        compiler_params=pltpu.CompilerParams(vmem_limit_bytes=STEP_LIMIT),
        name="put",
    )(place, *values, *extra)


def by_core(value, near, wide):
    def rule(x, z, y, c):
        move = near if c == 0 else wide
        if move is None:
            return None
        return x, (z + move[0]) % NZ, (y + move[1]) % NY, c

    return send(value, rule)


def gather_plane(block, place, extra, prepare):
    together = lax.optimization_barrier
    up, down, right, left = (1, 0), (-1, 0), (0, 1), (0, -1)
    up2, down2, right2 = (2, 0), (-2, 0), (0, 2)
    right2, up2, down2 = (0, 2), (2, 0), (-2, 0)
    near = [by_core(block, right, up), by_core(block, left, down), by_core(block, right2, up2), by_core(block, None, down2)]
    lower, upper, lower2, upper2 = together(tuple(near))
    head = jnp.stack([block, lower, lower2, upper])

    lower3, lower4, upper3 = by_core(lower, None, up2), by_core(lower2, None, up2), by_core(upper, None, down2)
    lead, lag = by_core(head, up, right), by_core(head, down, left)
    lead, lag, lower3, lower4, upper3 = together((lead, lag, lower3, lower4, upper3))
    third, fourth = choose(place, [lead, lag], [[lower3, lower4, upper2, upper3]] * 2)
    third, fourth, extra, head, lead, lag = together((third, fourth, extra, head, lead, lag))

    lead2, lag2 = by_core(third, up, right), by_core(fourth, down, left)
    extra = prepare(extra)
    ready = [(head, HEAD), (lead, LEAD), (lag, LAG1)]
    ready += [(other_core(v), from_other(w)) for v, w in ready]
    ready += [(third, TAIL), (core_to_core(third, 1), from_other(TAIL))]
    lead2, lag2, extra = together((lead2, lag2, extra))
    up_halves, down_halves = choose(place, [lead2, lag2], [lead, lag2], True)

    lead3 = [by_core(half, up, right) for half in up_halves]
    lag3 = [by_core(half, down, left) for half in down_halves]
    into = put(place, ready, None)
    lead3, lag3, lead2, lag2, into = together((lead3, lag3, lead2, lag2, into))

    far = by_core(lead3[0], up, None), by_core(lag3[1], down, None)
    ready = [(lead2, LEAD2), (lag2, LAG2)]
    into = put(place, ready + [(other_core(v), from_other(w)) for v, w in ready], into)
    ready = [(v, w) for v, w in zip([*lead3, *lag3], LEAD3 + LAG3)]
    ready += [(other_core(v), from_other(w)) for v, w in ready]
    far, into = together((far, into))
    for v, w in zip(far, FAR):
        ready += [(v, w), (core_to_core(v, 0), from_other(w))]
    return put(place, ready, into), extra


def choose_kernel(parts, place, *refs):
    values, outs = refs[:-parts], refs[-parts:]
    half = parts // 2
    rest = (len(values) - 2) // 2

    def fill(n, sources):
        for m in range(4):
            out = outs[n * half + (m // 2 if half == 2 else 0)]
            at = m % 2 if half == 2 else m
            out[at] = sources[0][m] if len(sources) == 1 else sources[m][...]

    for n in range(2):
        pl.when(place[2] == 0)(functools.partial(fill, n, values[n : n + 1]))
        pl.when(place[2] == 1)(functools.partial(fill, n, values[2 + n * rest : 2 + (n + 1) * rest]))


def choose(place, zero, one, in_two=False):
    one = [v if isinstance(v, list) else [v] for v in one]
    values = [*zero, *one[0], *one[1]]
    parts = 4 if in_two else 2
    shape = (2 if in_two else 4, *zero[0].shape[1:])
    vmem = pl.BlockSpec(memory_space=pltpu.VMEM)
    outs = pl.pallas_call(
        functools.partial(choose_kernel, parts),
        in_specs=[pl.BlockSpec(memory_space=pltpu.SMEM)] + [vmem] * len(values),
        out_specs=(vmem,) * parts,
        out_shape=(jax.ShapeDtypeStruct(shape, zero[0].dtype),) * parts,
        compiler_params=pltpu.CompilerParams(vmem_limit_bytes=STEP_LIMIT),
        name="choose",
    )(place, *values)
    return (outs[:2], outs[2:]) if in_two else outs


def core_to_core(value, source):
    return send(value, lambda x, z, y, c: (x, z, y, 1 - c) if c == source else None)


def rows_at(dz):
    return [(dz, dy) for dy in (0, -1, 2, 1)]


def column_at(dy, zs):
    return [(dz, dy) for dz in zs]


def in_halves(source, near, wide):
    return tuple((source, False, near[n : n + 2], wide[n : n + 2]) for n in (0, 2))


def from_other(where):
    return (where[0], True, *where[2:])


Z_HEAD, Z_TAIL = (0, -1, -2, 1), (-3, 4, 2, 3)
HEAD = (None, False, rows_at(0), column_at(0, Z_HEAD))
LEAD = (None, False, rows_at(-1), column_at(-1, Z_HEAD))
LAG1 = (None, False, rows_at(1), column_at(1, Z_HEAD))
TAIL = (1, False, column_at(0, Z_TAIL), column_at(0, Z_TAIL))
LEAD2 = (None, False, rows_at(-2), column_at(-1, Z_TAIL))
LAG2 = (None, False, rows_at(2), column_at(1, Z_TAIL))
LEAD3 = in_halves(None, rows_at(-3), column_at(2, Z_HEAD))
LAG3 = in_halves(None, rows_at(3), column_at(2, Z_TAIL))
FAR = in_halves(0, rows_at(4), rows_at(4))


def item_of(tick, x):
    return jnp.clip(tick - LAG * x, 0, ITEMS - 1)


def step_kernel(tick, which, meta, consts, env, *refs):
    refs = list(refs)
    arrived = refs.pop(0) if tick >= LAG else None
    both = refs[0]
    e_out, kept, hop, *swaps, current, early = refs[-5 - len(which) :]
    x, zl = meta[0], meta[1]
    turn = tick - LAG * x
    valid = (turn >= 0) & (turn < ITEMS)
    item = item_of(tick, x)
    k, own = lax.rem(item, 4), item // 4
    sec = 2 * zl + own
    target = meta[2 + 4 * k + sec]

    if tick == 0:
        e_out[...] = jnp.zeros_like(e_out)

    @pl.when(x == 0)
    def _():
        current[...] = env[item]

    if tick >= LAG:

        @pl.when(x != 0)
        def _():
            current[...] = arrived[...]

    @pl.when(valid)
    def _():
        def two_sites(pair, carry):
            for s in (2 * pair, 2 * pair + 1):
                middle = jnp.dot(current[...], both[s, target, :, :WIDE], preferred_element_type=jnp.float32).astype(jnp.bfloat16)
                total = consts[4 * s + k] * both[s, sec, :, WIDE:].astype(jnp.float32)
                for d in range(LOCAL):
                    cols = slice(d * BLK, (d + 1) * BLK)
                    total += lax.dot_general(both[s, sec, :, cols], middle[:, cols], FIRST_AXES, preferred_element_type=jnp.float32)
                new = total.astype(jnp.bfloat16)
                current[...] = new
                e_out[own, s] += consts[16 + 4 * s + k] * new.astype(jnp.float32)

            @pl.when(pair == 0)
            def _():
                early[...] = current[...]

            return carry

        lax.fori_loop(0, 2, two_sites, 0)
        hop[...] = current[...]

        @pl.when(zl == 0)
        def _():
            kept[item] = early[...]

        @pl.when(zl == 1)
        def _():
            kept[item] = current[...]

        for part, swap in zip(which, swaps):
            first, end = PARTS[part]
            inside = (item >= first) & (item < end)

            @pl.when(inside & (zl == 0))
            def _():
                swap[item - first] = current[...]

            @pl.when(inside & (zl == 1))
            def _():
                swap[item - first] = early[...]


def parts_at(tick):
    turns = [tick - LAG * x for x in range(NX)]
    return [n for n, (first, end) in enumerate(PARTS) if any(first <= turn < end for turn in turns)]


def step(tick, meta, consts, env, arrived, both, energy, kept, swaps):
    vmem, smem = pl.BlockSpec(memory_space=pltpu.VMEM), pl.BlockSpec(memory_space=pltpu.SMEM)
    which = parts_at(tick)
    operands = [env]
    if tick >= LAG:
        operands.append(arrived)
    operands += [both]
    aliases = {}
    if tick > 0:
        aliases = {2 + len(operands): 0, 3 + len(operands): 1}
        operands += [energy, kept]
    for n, part in enumerate(which):
        if part in swaps:
            aliases[2 + len(operands)] = 3 + n
            operands.append(swaps[part])
    energy, kept, hop, *outs = pl.pallas_call(
        functools.partial(step_kernel, tick, which),
        in_specs=[smem, smem] + [vmem] * len(operands),
        out_specs=(vmem,) * (3 + len(which)),
        out_shape=(
            pltpu.VMEM((2, 4, BLK, BLK), jnp.float32),
            pltpu.VMEM((ITEMS, BLK, BLK), jnp.bfloat16),
            pltpu.VMEM((BLK, BLK), jnp.bfloat16),
        )
        + tuple(pltpu.VMEM((PARTS[n][1] - PARTS[n][0], BLK, BLK), jnp.bfloat16) for n in which),
        scratch_shapes=[pltpu.VMEM((BLK, BLK), jnp.bfloat16)] * 2,
        input_output_aliases=aliases,
        compiler_params=pltpu.CompilerParams(vmem_limit_bytes=STEP_LIMIT),
        name="renormalize",
    )(meta, consts, *[held(v) for v in operands])
    return energy, kept, hop, dict(zip(which, outs))


def place_kernel(part, meta, *refs):
    other, out, sem = refs[0], refs[-2], refs[-1]
    zl = meta[1]
    first, end = PARTS[part]
    copies = []
    for n, item in enumerate(range(first, end)):
        copies.append(pltpu.make_async_copy(other.at[n], out.at[item % 4, 2 * (1 - zl) + item // 4], sem.at[n]))
    if part == 0:
        kept = refs[1]
        for item in range(ITEMS):
            copies.append(pltpu.make_async_copy(kept.at[item], out.at[item % 4, 2 * zl + item // 4], sem.at[ITEMS + item]))
    for copy in copies:
        copy.start()
    for copy in copies:
        copy.wait()


def place_items(part, meta, other, rest):
    vmem, hbm = pl.BlockSpec(memory_space=pltpu.VMEM), pl.BlockSpec(memory_space=pltpu.HBM)
    return pl.pallas_call(
        functools.partial(place_kernel, part),
        in_specs=[pl.BlockSpec(memory_space=pltpu.SMEM), vmem, vmem if part == 0 else hbm],
        out_specs=hbm,
        out_shape=pltpu.HBM((4, SECT, BLK, BLK), jnp.bfloat16),
        scratch_shapes=[pltpu.SemaphoreType.DMA((2 * ITEMS,))],
        input_output_aliases={} if part == 0 else {2: 0},
        compiler_params=pltpu.CompilerParams(vmem_limit_bytes=STEP_LIMIT),
        name="place_items",
    )(meta, other, rest)


def piece(value, axis, place, size):
    return lax.dynamic_slice_in_dim(value, place * size, size, axis)


def on_core(body, place, operands, shapes, out_hbm=False):
    vmem = pl.BlockSpec(memory_space=pltpu.VMEM)
    return pl.pallas_call(
        body,
        in_specs=[pl.BlockSpec(memory_space=pltpu.SMEM)] + [vmem] * len(operands),
        out_specs=(vmem,) * len(shapes),
        out_shape=tuple(jax.ShapeDtypeStruct(shape, dtype) for shape, dtype in shapes),
        compiler_params=pltpu.CompilerParams(vmem_limit_bytes=2 * STEP_LIMIT),
        name=body.__name__,
    )(place, *operands)


HALF, QUARTER = BLK // 2, BLK // 8
AROUND = (2, 1, -1)
ALONG = (4, 3, -3, 2, -2, 1, -1)


def rows_of(place, count):
    return pl.ds(pl.multiple_of(place * count, count), count)


def halve(place, energy, out):
    out[...] = energy[:, :, rows_of(1 - place[2], HALF), :].astype(jnp.bfloat16)


def quarter(place, energy, got, own, *outs):
    own_rows, y = rows_of(place[2], HALF), place[1]

    def total(at):
        first = pl.multiple_of(place[2] * HALF + at * QUARTER, QUARTER)
        return energy[:, :, pl.ds(first, QUARTER), :] + got[:, :, rows_of(at, QUARTER), :].astype(jnp.float32)

    own[...] = total(y)
    for out, step in zip(outs, AROUND):
        out[...] = total(lax.rem(y + NY + step, NY)).astype(jnp.bfloat16)


def by_lane(place, own, first, second, third, mine, near, far):
    zl = place[3]

    def total(lane):
        at = pl.ds(2 * lane, 2)
        return own[:, at] + (first[:, at].astype(jnp.float32) + second[:, at].astype(jnp.float32) + third[:, at].astype(jnp.float32))

    mine[...] = total(zl)
    near[...] = mine[...].astype(jnp.bfloat16)
    far[...] = total(1 - zl).astype(jnp.bfloat16)


def line_up(place, mine, *refs):
    out, zl = refs[-1], place[3]

    def total(parity):
        return sum(ref[...].astype(jnp.float32) for ref, step in zip(refs, ALONG) if step % 2 == parity)

    same, other = mine[...] + total(0), total(1)
    for n in range(2):
        for sector in range(2):
            out[n, 2 * zl + sector] = same[sector, n].astype(jnp.bfloat16)
            out[n, 2 * (1 - zl) + sector] = other[sector, n].astype(jnp.bfloat16)


def join_y(place, own, first, second, third, out):
    out[:, :, rows_of(place[1], QUARTER), :] = own[...]
    for ref, step in zip((first, second, third), AROUND):
        out[:, :, rows_of(lax.rem(place[1] + NY - step, NY), QUARTER), :] = ref[...]


def join_core(place, own, other, out):
    out[:, :, rows_of(place[2], HALF), :] = own[...].astype(jnp.float32)
    out[:, :, rows_of(1 - place[2], HALF), :] = other[...].astype(jnp.float32)


def reduce_energy(energy, place, meta, kept, ended):
    bf16, f32 = jnp.bfloat16, jnp.float32
    energy = held(energy)
    (theirs,) = on_core(halve, place, [energy], [((2, 4, HALF, BLK), bf16)])
    got = other_core(theirs)
    shape = (2, 4, QUARTER, BLK)
    own, *parts = on_core(quarter, place, [energy, got], [(shape, f32)] + [(shape, bf16)] * 3)
    parts = [along_y(part, step) for part, step in zip(parts, AROUND)]
    shape = (2, 2, QUARTER, BLK)
    mine, near, far = on_core(by_lane, place, [own, *parts], [(shape, f32)] + [(shape, bf16)] * 2)
    parts = [along_z(far if step % 2 else near, step) for step in ALONG]
    out = place_items(0, meta, other_lane(ended[0]), kept)
    parts, late, out = lax.optimization_barrier((parts, ended[1], out))
    late = other_lane(late)
    (flat,) = on_core(line_up, place, [mine, *parts], [((2, 4, QUARTER, BLK), bf16)])
    parts = [along_y(flat, step) for step in AROUND]
    parts[-1], late = lax.optimization_barrier((parts[-1], late))
    out = place_items(1, meta, late, out)
    (flat,) = on_core(join_y, place, [flat, *parts], [((2, 4, HALF, BLK), bf16)])
    (flat,) = on_core(join_core, place, [flat, other_core(flat)], [((2, 4, BLK, BLK), f32)])
    return out[None], flat


def pick_kernel(pair_of, coupling, weight, out):
    for s in range(2):
        for k in range(4):
            out[4 * s + k] = coupling[s, pair_of[k]]
            out[8 + 4 * s + k] = weight[s, pair_of[k]]


def pick(pair_of, coupling, weight):
    smem = pl.BlockSpec(memory_space=pltpu.SMEM)
    return pl.pallas_call(
        pick_kernel,
        in_specs=[smem] * 3,
        out_specs=smem,
        out_shape=jax.ShapeDtypeStruct((16,), jnp.float32),
        name="pick",
    )(pair_of, coupling, weight)


def local(environment, rotations, site_terms, pair_of, targets, coupling, energy_coef):
    sweep, op = lax.axis_index("sweep"), lax.axis_index("op")
    x, zl = sweep // 2, sweep % 2
    zh, y, c = op // 8, (op // 2) % 4, op % 2
    z = 2 * zh + zl

    wide = jnp.concatenate([rotations, site_terms], axis=3)
    mine, theirs = wide[c], wide[1 - c]
    got = other_core(theirs)
    block = jnp.where(c == 0, jnp.concatenate([mine, got], axis=1), jnp.concatenate([got, mine], axis=1))
    place = jnp.stack([z, y, c, zl]).astype(jnp.int32)

    def prepare(operands):
        pair_of, targets, coupling, energy_coef, environment = operands
        values = pick(pair_of, coupling, energy_coef).reshape(2, 8)
        got = other_lane(values)
        consts = jnp.where(zl == 0, jnp.concatenate([values, got], axis=1), jnp.concatenate([got, values], axis=1)).reshape(-1)
        meta = jnp.concatenate([jnp.stack([x, zl]).astype(jnp.int32), targets.reshape(-1)])
        env = piece(environment, 1, zl, 2).swapaxes(0, 1).reshape(ITEMS, BLK, BLK)
        return consts, meta, env

    operands = (pair_of, targets, coupling, energy_coef, environment)
    both, (consts, meta, env) = gather_plane(block, place, operands, prepare)

    energy, kept, swaps, hops, ended = None, None, {}, [], {}
    for tick in range(TICKS):
        arrived = hops[tick - LAG] if tick >= LAG else None
        energy, kept, hop, swaps = step(tick, meta, consts, env, arrived, both, energy, kept, swaps)
        hops.append(next_stage(hop) if tick < TICKS - LAG else None)
        for part in swaps:
            if part not in parts_at(tick + 1):
                ended[part] = swaps[part]
    return reduce_energy(energy, place, meta, kept, ended)


def solution(mesh):
    return jax.shard_map(
        local,
        mesh=mesh,
        in_specs=(
            P("op", None, None, None),
            P("sweep", None, "op", None),
            P("sweep", None, "op", None),
            P("op"),
            P("op", None),
            P("sweep", None),
            P("sweep", None),
        ),
        out_specs=(P("sweep", "op", None, None, None), P("sweep", None, None, None)),
        check_vma=False,
    )
```

```python
import functools

import jax
import jax.numpy as jnp
from jax import lax
from jax.experimental import pallas as pl
from jax.experimental.pallas import tpu as pltpu
from jax.sharding import PartitionSpec as P

NX, NZL, NZH, NY, NC = 4, 2, 4, 4, 2
NZ = NZL * NZH
SECT, BLK, LOCAL = 4, 256, 4
WIDE = LOCAL * BLK
BOTH = WIDE + BLK
ITEMS = 8
SPLIT = 5
PARTS = ((0, SPLIT), (SPLIT, ITEMS))
LAG = 2
TICKS = ITEMS + LAG * (NX - 1)
STEP_LIMIT = 8 * 1024 * 1024

FIRST_AXES = (((0,), (0,)), ((), ()))
AXES = ("sweep", "op")


def number(x, z, y, c):
    zh, zl = z // 2, z % 2
    return (x * NZL + zl) * (NZH * NY * NC) + (zh * NY + y) * NC + c


def send(value, rule):
    pairs = []
    for x in range(NX):
        for z in range(NZ):
            for y in range(NY):
                for c in range(NC):
                    to = rule(x, z, y, c)
                    if to is not None:
                        pairs.append((number(x, z, y, c), number(*to)))
    return lax.ppermute(value, AXES, pairs)


def along_y(value, step):
    return send(value, lambda x, z, y, c: (x, z, (y + step) % NY, c))


def along_z(value, step):
    return send(value, lambda x, z, y, c: (x, (z + step) % NZ, y, c))


def other_core(value):
    return send(value, lambda x, z, y, c: (x, z, y, 1 - c))


def other_lane(value):
    return send(value, lambda x, z, y, c: (x, z ^ 1, y, c))


def next_stage(value):
    return send(value, lambda x, z, y, c: (x + 1, z, y, c) if x + 1 < NX else None)


def after(value, *others):
    return lax.optimization_barrier((value, others))[0]


def held(value):
    return pltpu.with_memory_space_constraint(value, pltpu.VMEM)


def put_kernel(layout, place, *refs):
    both, sem = refs[-2:]
    z, y, c = place[0], place[1], place[2]
    copies = []
    for n, (ref, (source, other, near, wide)) in enumerate(zip(refs, layout)):
        core = 1 - c if other else c
        does = None if source is None else core == source
        for lead, (p, q) in enumerate(zip(near, wide)):
            zs = lax.rem(z + NZ + jnp.where(core == 0, p[0], q[0]), NZ)
            ys = lax.rem(y + NY + jnp.where(core == 0, p[1], q[1]), NY)
            row = pl.ds(pl.multiple_of(((zs // 2) * NY + ys) * 16, 16), 16)
            to = both.at[2 * lax.rem(zs, 2) + core, :, row, :]
            copies.append((does, pltpu.make_async_copy(ref.at[lead], to, sem.at[n, lead])))
    for does, copy in copies:
        if does is None:
            copy.start()
        else:
            pl.when(does)(copy.start)
    for does, copy in copies:
        if does is None:
            copy.wait()
        else:
            pl.when(does)(copy.wait)


def put(place, pieces, into):
    layout = [where for _, where in pieces]
    values = [value for value, _ in pieces]
    count = len(pieces)
    vmem, anywhere = pl.BlockSpec(memory_space=pltpu.VMEM), pl.BlockSpec(memory_space=pl.ANY)
    extra = [] if into is None else [held(into)]
    return pl.pallas_call(
        functools.partial(put_kernel, layout),
        out_shape=pltpu.VMEM((4, SECT, BLK, BOTH), jnp.bfloat16),
        in_specs=[pl.BlockSpec(memory_space=pltpu.SMEM)] + [anywhere] * count + [vmem] * len(extra),
        out_specs=vmem,
        scratch_shapes=[pltpu.SemaphoreType.DMA((count, 4))],
        input_output_aliases={} if into is None else {1 + count: 0},
        compiler_params=pltpu.CompilerParams(vmem_limit_bytes=STEP_LIMIT),
        name="put",
    )(place, *values, *extra)


def by_core(value, near, wide):
    def rule(x, z, y, c):
        move = near if c == 0 else wide
        if move is None:
            return None
        return x, (z + move[0]) % NZ, (y + move[1]) % NY, c

    return send(value, rule)


def gather_plane(block, place, extra, prepare):
    together = lax.optimization_barrier
    up, down, right, left = (1, 0), (-1, 0), (0, 1), (0, -1)
    up2, down2, right2 = (2, 0), (-2, 0), (0, 2)
    right2, up2, down2 = (0, 2), (2, 0), (-2, 0)
    near = [by_core(block, right, up), by_core(block, left, down), by_core(block, right2, up2), by_core(block, None, down2)]
    lower, upper, lower2, upper2 = together(tuple(near))
    head = jnp.stack([block, lower, lower2, upper])

    lower3, lower4, upper3 = by_core(lower, None, up2), by_core(lower2, None, up2), by_core(upper, None, down2)
    lead, lag = by_core(head, up, right), by_core(head, down, left)
    lead, lag, lower3, lower4, upper3 = together((lead, lag, lower3, lower4, upper3))
    third, fourth = choose(place, [lead, lag], [[lower3, lower4, upper2, upper3]] * 2)
    third, fourth, extra, head, lead, lag = together((third, fourth, extra, head, lead, lag))

    lead2, lag2 = by_core(third, up, right), by_core(fourth, down, left)
    extra = prepare(extra)
    ready = [(head, HEAD), (lead, LEAD), (lag, LAG1)]
    ready += [(other_core(v), from_other(w)) for v, w in ready]
    ready += [(third, TAIL), (core_to_core(third, 1), from_other(TAIL))]
    lead2, lag2, extra = together((lead2, lag2, extra))
    up_halves, down_halves = choose(place, [lead2, lag2], [lead, lag2], True)

    lead3 = [by_core(half, up, right) for half in up_halves]
    lag3 = [by_core(half, down, left) for half in down_halves]
    into = put(place, ready, None)
    lead3, lag3, lead2, lag2, into = together((lead3, lag3, lead2, lag2, into))

    far = by_core(lead3[0], up, None), by_core(lag3[1], down, None)
    ready = [(lead2, LEAD2), (lag2, LAG2)]
    into = put(place, ready + [(other_core(v), from_other(w)) for v, w in ready], into)
    ready = [(v, w) for v, w in zip([*lead3, *lag3], LEAD3 + LAG3)]
    ready += [(other_core(v), from_other(w)) for v, w in ready]
    far, into = together((far, into))
    for v, w in zip(far, FAR):
        ready += [(v, w), (core_to_core(v, 0), from_other(w))]
    return put(place, ready, into), extra


def choose_kernel(parts, place, *refs):
    values, outs = refs[:-parts], refs[-parts:]
    half = parts // 2
    rest = (len(values) - 2) // 2

    def fill(n, sources):
        for m in range(4):
            out = outs[n * half + (m // 2 if half == 2 else 0)]
            at = m % 2 if half == 2 else m
            out[at] = sources[0][m] if len(sources) == 1 else sources[m][...]

    for n in range(2):
        pl.when(place[2] == 0)(functools.partial(fill, n, values[n : n + 1]))
        pl.when(place[2] == 1)(functools.partial(fill, n, values[2 + n * rest : 2 + (n + 1) * rest]))


def choose(place, zero, one, in_two=False):
    one = [v if isinstance(v, list) else [v] for v in one]
    values = [*zero, *one[0], *one[1]]
    parts = 4 if in_two else 2
    shape = (2 if in_two else 4, *zero[0].shape[1:])
    vmem = pl.BlockSpec(memory_space=pltpu.VMEM)
    outs = pl.pallas_call(
        functools.partial(choose_kernel, parts),
        in_specs=[pl.BlockSpec(memory_space=pltpu.SMEM)] + [vmem] * len(values),
        out_specs=(vmem,) * parts,
        out_shape=(jax.ShapeDtypeStruct(shape, zero[0].dtype),) * parts,
        compiler_params=pltpu.CompilerParams(vmem_limit_bytes=STEP_LIMIT),
        name="choose",
    )(place, *values)
    return (outs[:2], outs[2:]) if in_two else outs


def core_to_core(value, source):
    return send(value, lambda x, z, y, c: (x, z, y, 1 - c) if c == source else None)


def rows_at(dz):
    return [(dz, dy) for dy in (0, -1, 2, 1)]


def column_at(dy, zs):
    return [(dz, dy) for dz in zs]


def in_halves(source, near, wide):
    return tuple((source, False, near[n : n + 2], wide[n : n + 2]) for n in (0, 2))


def from_other(where):
    return (where[0], True, *where[2:])


Z_HEAD, Z_TAIL = (0, -1, -2, 1), (-3, 4, 2, 3)
HEAD = (None, False, rows_at(0), column_at(0, Z_HEAD))
LEAD = (None, False, rows_at(-1), column_at(-1, Z_HEAD))
LAG1 = (None, False, rows_at(1), column_at(1, Z_HEAD))
TAIL = (1, False, column_at(0, Z_TAIL), column_at(0, Z_TAIL))
LEAD2 = (None, False, rows_at(-2), column_at(-1, Z_TAIL))
LAG2 = (None, False, rows_at(2), column_at(1, Z_TAIL))
LEAD3 = in_halves(None, rows_at(-3), column_at(2, Z_HEAD))
LAG3 = in_halves(None, rows_at(3), column_at(2, Z_TAIL))
FAR = in_halves(0, rows_at(4), rows_at(4))


def item_of(tick, x):
    return jnp.clip(tick - LAG * x, 0, ITEMS - 1)


def step_kernel(tick, which, meta, consts, env, *refs):
    refs = list(refs)
    arrived = refs.pop(0) if tick >= LAG else None
    both = refs[0]
    e_out, kept, hop, *swaps, current, early = refs[-5 - len(which) :]
    x, zl = meta[0], meta[1]
    turn = tick - LAG * x
    valid = (turn >= 0) & (turn < ITEMS)
    item = item_of(tick, x)
    k, own = lax.rem(item, 4), item // 4
    sec = 2 * zl + own
    target = meta[2 + 4 * k + sec]

    if tick == 0:
        e_out[...] = jnp.zeros_like(e_out)

    @pl.when(x == 0)
    def _():
        current[...] = env[item]

    if tick >= LAG:

        @pl.when(x != 0)
        def _():
            current[...] = arrived[...]

    @pl.when(valid)
    def _():
        def two_sites(pair, carry):
            for s in (2 * pair, 2 * pair + 1):
                middle = jnp.dot(current[...], both[s, target, :, :WIDE], preferred_element_type=jnp.float32).astype(jnp.bfloat16)
                total = consts[4 * s + k] * both[s, sec, :, WIDE:].astype(jnp.float32)
                for d in range(LOCAL):
                    cols = slice(d * BLK, (d + 1) * BLK)
                    total += lax.dot_general(both[s, sec, :, cols], middle[:, cols], FIRST_AXES, preferred_element_type=jnp.float32)
                new = total.astype(jnp.bfloat16)
                current[...] = new
                e_out[own, s] += consts[16 + 4 * s + k] * new.astype(jnp.float32)

            @pl.when(pair == 0)
            def _():
                early[...] = current[...]

            return carry

        lax.fori_loop(0, 2, two_sites, 0)
        hop[...] = current[...]

        @pl.when(zl == 0)
        def _():
            kept[item] = early[...]

        @pl.when(zl == 1)
        def _():
            kept[item] = current[...]

        for part, swap in zip(which, swaps):
            first, end = PARTS[part]
            inside = (item >= first) & (item < end)

            @pl.when(inside & (zl == 0))
            def _():
                swap[item - first] = current[...]

            @pl.when(inside & (zl == 1))
            def _():
                swap[item - first] = early[...]


def parts_at(tick):
    turns = [tick - LAG * x for x in range(NX)]
    return [n for n, (first, end) in enumerate(PARTS) if any(first <= turn < end for turn in turns)]


def step(tick, meta, consts, env, arrived, both, energy, kept, swaps):
    vmem, smem = pl.BlockSpec(memory_space=pltpu.VMEM), pl.BlockSpec(memory_space=pltpu.SMEM)
    which = parts_at(tick)
    operands = [env]
    if tick >= LAG:
        operands.append(arrived)
    operands += [both]
    aliases = {}
    if tick > 0:
        aliases = {2 + len(operands): 0, 3 + len(operands): 1}
        operands += [energy, kept]
    for n, part in enumerate(which):
        if part in swaps:
            aliases[2 + len(operands)] = 3 + n
            operands.append(swaps[part])
    energy, kept, hop, *outs = pl.pallas_call(
        functools.partial(step_kernel, tick, which),
        in_specs=[smem, smem] + [vmem] * len(operands),
        out_specs=(vmem,) * (3 + len(which)),
        out_shape=(
            pltpu.VMEM((2, 4, BLK, BLK), jnp.float32),
            pltpu.VMEM((ITEMS, BLK, BLK), jnp.bfloat16),
            pltpu.VMEM((BLK, BLK), jnp.bfloat16),
        )
        + tuple(pltpu.VMEM((PARTS[n][1] - PARTS[n][0], BLK, BLK), jnp.bfloat16) for n in which),
        scratch_shapes=[pltpu.VMEM((BLK, BLK), jnp.bfloat16)] * 2,
        input_output_aliases=aliases,
        compiler_params=pltpu.CompilerParams(vmem_limit_bytes=STEP_LIMIT),
        name="renormalize",
    )(meta, consts, *[held(v) for v in operands])
    return energy, kept, hop, dict(zip(which, outs))


def place_kernel(part, meta, *refs):
    other, out, sem = refs[0], refs[-2], refs[-1]
    zl = meta[1]
    first, end = PARTS[part]
    copies = []
    for n, item in enumerate(range(first, end)):
        copies.append(pltpu.make_async_copy(other.at[n], out.at[item % 4, 2 * (1 - zl) + item // 4], sem.at[n]))
    if part == 0:
        kept = refs[1]
        for item in range(ITEMS):
            copies.append(pltpu.make_async_copy(kept.at[item], out.at[item % 4, 2 * zl + item // 4], sem.at[ITEMS + item]))
    for copy in copies:
        copy.start()
    for copy in copies:
        copy.wait()


def place_items(part, meta, other, rest):
    vmem, hbm = pl.BlockSpec(memory_space=pltpu.VMEM), pl.BlockSpec(memory_space=pltpu.HBM)
    return pl.pallas_call(
        functools.partial(place_kernel, part),
        in_specs=[pl.BlockSpec(memory_space=pltpu.SMEM), vmem, vmem if part == 0 else hbm],
        out_specs=hbm,
        out_shape=pltpu.HBM((4, SECT, BLK, BLK), jnp.bfloat16),
        scratch_shapes=[pltpu.SemaphoreType.DMA((2 * ITEMS,))],
        input_output_aliases={} if part == 0 else {2: 0},
        compiler_params=pltpu.CompilerParams(vmem_limit_bytes=STEP_LIMIT),
        name="place_items",
    )(meta, other, rest)


def piece(value, axis, place, size):
    return lax.dynamic_slice_in_dim(value, place * size, size, axis)


def on_core(body, place, operands, shapes, out_hbm=False):
    vmem = pl.BlockSpec(memory_space=pltpu.VMEM)
    return pl.pallas_call(
        body,
        in_specs=[pl.BlockSpec(memory_space=pltpu.SMEM)] + [vmem] * len(operands),
        out_specs=(vmem,) * len(shapes),
        out_shape=tuple(jax.ShapeDtypeStruct(shape, dtype) for shape, dtype in shapes),
        compiler_params=pltpu.CompilerParams(vmem_limit_bytes=2 * STEP_LIMIT),
        name=body.__name__,
    )(place, *operands)


HALF, QUARTER = BLK // 2, BLK // 8
AROUND = (2, 1, -1)
ALONG = (4, 3, -3, 2, -2, 1, -1)


def rows_of(place, count):
    return pl.ds(pl.multiple_of(place * count, count), count)


def halve(place, energy, out):
    out[...] = energy[:, :, rows_of(1 - place[2], HALF), :].astype(jnp.bfloat16)


def quarter(place, energy, got, own, *outs):
    own_rows, y = rows_of(place[2], HALF), place[1]

    def total(at):
        first = pl.multiple_of(place[2] * HALF + at * QUARTER, QUARTER)
        return energy[:, :, pl.ds(first, QUARTER), :] + got[:, :, rows_of(at, QUARTER), :].astype(jnp.float32)

    own[...] = total(y)
    for out, step in zip(outs, AROUND):
        out[...] = total(lax.rem(y + NY + step, NY)).astype(jnp.bfloat16)


def by_lane(place, own, first, second, third, mine, near, far):
    zl = place[3]

    def total(lane):
        at = pl.ds(2 * lane, 2)
        return own[:, at] + (first[:, at].astype(jnp.float32) + second[:, at].astype(jnp.float32) + third[:, at].astype(jnp.float32))

    mine[...] = total(zl)
    near[...] = mine[...].astype(jnp.bfloat16)
    far[...] = total(1 - zl).astype(jnp.bfloat16)


def line_up(place, mine, *refs):
    out, zl = refs[-1], place[3]

    def total(parity):
        return sum(ref[...].astype(jnp.float32) for ref, step in zip(refs, ALONG) if step % 2 == parity)

    same, other = mine[...] + total(0), total(1)
    for n in range(2):
        for sector in range(2):
            out[n, 2 * zl + sector] = same[sector, n].astype(jnp.bfloat16)
            out[n, 2 * (1 - zl) + sector] = other[sector, n].astype(jnp.bfloat16)


def join_y(place, own, first, second, third, out):
    out[:, :, rows_of(place[1], QUARTER), :] = own[...]
    for ref, step in zip((first, second, third), AROUND):
        out[:, :, rows_of(lax.rem(place[1] + NY - step, NY), QUARTER), :] = ref[...]


def join_core(place, own, other, out):
    out[:, :, rows_of(place[2], HALF), :] = own[...].astype(jnp.float32)
    out[:, :, rows_of(1 - place[2], HALF), :] = other[...].astype(jnp.float32)


def reduce_energy(energy, place, meta, kept, ended):
    bf16, f32 = jnp.bfloat16, jnp.float32
    energy = held(energy)
    (theirs,) = on_core(halve, place, [energy], [((2, 4, HALF, BLK), bf16)])
    got = other_core(theirs)
    shape = (2, 4, QUARTER, BLK)
    own, *parts = on_core(quarter, place, [energy, got], [(shape, f32)] + [(shape, bf16)] * 3)
    parts = [along_y(part, step) for part, step in zip(parts, AROUND)]
    shape = (2, 2, QUARTER, BLK)
    mine, near, far = on_core(by_lane, place, [own, *parts], [(shape, f32)] + [(shape, bf16)] * 2)
    parts = [along_z(far if step % 2 else near, step) for step in ALONG]
    out = place_items(0, meta, other_lane(ended[0]), kept)
    parts, late, out = lax.optimization_barrier((parts, ended[1], out))
    late = other_lane(late)
    (flat,) = on_core(line_up, place, [mine, *parts], [((2, 4, QUARTER, BLK), bf16)])
    parts = [along_y(flat, step) for step in AROUND]
    parts[-1], late = lax.optimization_barrier((parts[-1], late))
    out = place_items(1, meta, late, out)
    (flat,) = on_core(join_y, place, [flat, *parts], [((2, 4, HALF, BLK), bf16)])
    (flat,) = on_core(join_core, place, [flat, other_core(flat)], [((2, 4, BLK, BLK), f32)])
    return out[None], flat


def pick_kernel(pair_of, coupling, weight, out):
    for s in range(2):
        for k in range(4):
            out[4 * s + k] = coupling[s, pair_of[k]]
            out[8 + 4 * s + k] = weight[s, pair_of[k]]


def pick(pair_of, coupling, weight):
    smem = pl.BlockSpec(memory_space=pltpu.SMEM)
    return pl.pallas_call(
        pick_kernel,
        in_specs=[smem] * 3,
        out_specs=smem,
        out_shape=jax.ShapeDtypeStruct((16,), jnp.float32),
        name="pick",
    )(pair_of, coupling, weight)


def local(environment, rotations, site_terms, pair_of, targets, coupling, energy_coef):
    sweep, op = lax.axis_index("sweep"), lax.axis_index("op")
    x, zl = sweep // 2, sweep % 2
    zh, y, c = op // 8, (op // 2) % 4, op % 2
    z = 2 * zh + zl

    mine, theirs = (rotations[c], site_terms[c]), (rotations[1 - c], site_terms[1 - c])
    got = other_core(theirs[0]), other_core(theirs[1])
    low, high = [[jnp.where(c == n, a, b) for a, b in zip(mine, got)] for n in (0, 1)]
    block = jnp.concatenate([jnp.concatenate([low[n], high[n]], axis=1) for n in (0, 1)], axis=2)
    place = jnp.stack([z, y, c, zl]).astype(jnp.int32)

    def prepare(operands):
        pair_of, targets, coupling, energy_coef, environment = operands
        values = pick(pair_of, coupling, energy_coef).reshape(2, 8)
        got = other_lane(values)
        consts = jnp.where(zl == 0, jnp.concatenate([values, got], axis=1), jnp.concatenate([got, values], axis=1)).reshape(-1)
        meta = jnp.concatenate([jnp.stack([x, zl]).astype(jnp.int32), targets.reshape(-1)])
        env = piece(environment, 1, zl, 2).swapaxes(0, 1).reshape(ITEMS, BLK, BLK)
        return consts, meta, env

    operands = (pair_of, targets, coupling, energy_coef, environment)
    both, (consts, meta, env) = gather_plane(block, place, operands, prepare)

    energy, kept, swaps, hops, ended = None, None, {}, [], {}
    for tick in range(TICKS):
        arrived = hops[tick - LAG] if tick >= LAG else None
        energy, kept, hop, swaps = step(tick, meta, consts, env, arrived, both, energy, kept, swaps)
        hops.append(next_stage(hop) if tick < TICKS - LAG else None)
        for part in swaps:
            if part not in parts_at(tick + 1):
                ended[part] = swaps[part]
    return reduce_energy(energy, place, meta, kept, ended)


def solution(mesh):
    return jax.shard_map(
        local,
        mesh=mesh,
        in_specs=(
            P("op", None, None, None),
            P("sweep", None, "op", None),
            P("sweep", None, "op", None),
            P("op"),
            P("op", None),
            P("sweep", None),
            P("sweep", None),
        ),
        out_specs=(P("sweep", "op", None, None, None), P("sweep", None, None, None)),
        check_vma=False,
    )
```

```python
import functools

import jax
import jax.numpy as jnp
from jax import lax
from jax.experimental import pallas as pl
from jax.experimental.pallas import tpu as pltpu
from jax.sharding import PartitionSpec as P

NX, NZL, NZH, NY, NC = 4, 2, 4, 4, 2
NZ = NZL * NZH
SECT, BLK, LOCAL = 4, 256, 4
WIDE = LOCAL * BLK
BOTH = WIDE + BLK
ITEMS = 8
SPLIT = 4
PARTS = ((0, SPLIT), (SPLIT, ITEMS))
LAG = 2
TICKS = ITEMS + LAG * (NX - 1)
STEP_LIMIT = 8 * 1024 * 1024

FIRST_AXES = (((0,), (0,)), ((), ()))
AXES = ("sweep", "op")


def number(x, z, y, c):
    zh, zl = z // 2, z % 2
    return (x * NZL + zl) * (NZH * NY * NC) + (zh * NY + y) * NC + c


def send(value, rule):
    pairs = []
    for x in range(NX):
        for z in range(NZ):
            for y in range(NY):
                for c in range(NC):
                    to = rule(x, z, y, c)
                    if to is not None:
                        pairs.append((number(x, z, y, c), number(*to)))
    return lax.ppermute(value, AXES, pairs)


def along_y(value, step):
    return send(value, lambda x, z, y, c: (x, z, (y + step) % NY, c))


def along_z(value, step):
    return send(value, lambda x, z, y, c: (x, (z + step) % NZ, y, c))


def other_core(value):
    return send(value, lambda x, z, y, c: (x, z, y, 1 - c))


def other_lane(value):
    return send(value, lambda x, z, y, c: (x, z ^ 1, y, c))


def next_stage(value):
    return send(value, lambda x, z, y, c: (x + 1, z, y, c) if x + 1 < NX else None)


def after(value, *others):
    return lax.optimization_barrier((value, others))[0]


def held(value):
    return pltpu.with_memory_space_constraint(value, pltpu.VMEM)


def put_kernel(layout, place, *refs):
    both, sem = refs[-2:]
    z, y, c = place[0], place[1], place[2]
    copies = []
    for n, (ref, (source, other, near, wide)) in enumerate(zip(refs, layout)):
        core = 1 - c if other else c
        does = None if source is None else core == source
        for lead, (p, q) in enumerate(zip(near, wide)):
            zs = lax.rem(z + NZ + jnp.where(core == 0, p[0], q[0]), NZ)
            ys = lax.rem(y + NY + jnp.where(core == 0, p[1], q[1]), NY)
            row = pl.ds(pl.multiple_of(((zs // 2) * NY + ys) * 16, 16), 16)
            to = both.at[2 * lax.rem(zs, 2) + core, :, row, :]
            copies.append((does, pltpu.make_async_copy(ref.at[lead], to, sem.at[n, lead])))
    for does, copy in copies:
        if does is None:
            copy.start()
        else:
            pl.when(does)(copy.start)
    for does, copy in copies:
        if does is None:
            copy.wait()
        else:
            pl.when(does)(copy.wait)


def put(place, pieces, into):
    layout = [where for _, where in pieces]
    values = [value for value, _ in pieces]
    count = len(pieces)
    vmem, anywhere = pl.BlockSpec(memory_space=pltpu.VMEM), pl.BlockSpec(memory_space=pl.ANY)
    extra = [] if into is None else [held(into)]
    return pl.pallas_call(
        functools.partial(put_kernel, layout),
        out_shape=pltpu.VMEM((4, SECT, BLK, BOTH), jnp.bfloat16),
        in_specs=[pl.BlockSpec(memory_space=pltpu.SMEM)] + [anywhere] * count + [vmem] * len(extra),
        out_specs=vmem,
        scratch_shapes=[pltpu.SemaphoreType.DMA((count, 4))],
        input_output_aliases={} if into is None else {1 + count: 0},
        compiler_params=pltpu.CompilerParams(vmem_limit_bytes=STEP_LIMIT),
        name="put",
    )(place, *values, *extra)


def by_core(value, near, wide):
    def rule(x, z, y, c):
        move = near if c == 0 else wide
        if move is None:
            return None
        return x, (z + move[0]) % NZ, (y + move[1]) % NY, c

    return send(value, rule)


def gather_plane(block, place, extra, prepare):
    together = lax.optimization_barrier
    up, down, right, left = (1, 0), (-1, 0), (0, 1), (0, -1)
    up2, down2, right2 = (2, 0), (-2, 0), (0, 2)
    right2, up2, down2 = (0, 2), (2, 0), (-2, 0)
    near = [by_core(block, right, up), by_core(block, left, down), by_core(block, right2, up2), by_core(block, None, down2)]
    lower, upper, lower2, upper2 = together(tuple(near))
    head = jnp.stack([block, lower, lower2, upper])

    lower3, lower4, upper3 = by_core(lower, None, up2), by_core(lower2, None, up2), by_core(upper, None, down2)
    lead, lag = by_core(head, up, right), by_core(head, down, left)
    lead, lag, lower3, lower4, upper3 = together((lead, lag, lower3, lower4, upper3))
    third, fourth = choose(place, [lead, lag], [[lower3, lower4, upper2, upper3]] * 2)
    third, fourth, extra, head, lead, lag = together((third, fourth, extra, head, lead, lag))

    lead2, lag2 = by_core(third, up, right), by_core(fourth, down, left)
    extra = prepare(extra)
    ready = [(head, HEAD), (lead, LEAD), (lag, LAG1)]
    ready += [(other_core(v), from_other(w)) for v, w in ready]
    ready += [(third, TAIL), (core_to_core(third, 1), from_other(TAIL))]
    lead2, lag2, extra = together((lead2, lag2, extra))
    (third2,) = choose(place, [lead2], [lead])

    lead3, lag3 = by_core(third2, up, right), by_core(lag2, down, left)
    into = put(place, ready, None)
    lead3, lag3, lead2, lag2, into = together((lead3, lag3, lead2, lag2, into))

    first, last = ends(lead3, lag3)
    far = by_core(first, up, None), by_core(last, down, None)
    ready = [(lead2, LEAD2), (lag2, LAG2)]
    into = put(place, ready + [(other_core(v), from_other(w)) for v, w in ready], into)
    ready = [(lead3, LEAD3), (lag3, LAG3)]
    ready += [(other_core(v), from_other(w)) for v, w in ready]
    far, into = together((far, into))
    for v, w in zip(far, FAR):
        ready += [(v, w), (core_to_core(v, 0), from_other(w))]
    return put(place, ready, into), extra


def ends_kernel(lead, lag, first, last):
    first[...] = lead[:2]
    last[...] = lag[2:]


def ends(lead, lag):
    vmem = pl.BlockSpec(memory_space=pltpu.VMEM)
    half = jax.ShapeDtypeStruct((2, *lead.shape[1:]), lead.dtype)
    return pl.pallas_call(
        ends_kernel,
        in_specs=[vmem, vmem],
        out_specs=(vmem, vmem),
        out_shape=(half, half),
        compiler_params=pltpu.CompilerParams(vmem_limit_bytes=STEP_LIMIT),
        name="ends",
    )(lead, lag)


def choose_kernel(parts, place, *refs):
    values, outs = refs[:-parts], refs[-parts:]
    rest = (len(values) - parts) // parts

    def fill(out, sources):
        for m in range(4):
            out[m] = sources[0][m] if len(sources) == 1 else sources[m][...]

    for n, out in enumerate(outs):
        pl.when(place[2] == 0)(functools.partial(fill, out, values[n : n + 1]))
        pl.when(place[2] == 1)(functools.partial(fill, out, values[parts + n * rest : parts + (n + 1) * rest]))


def choose(place, zero, one):
    blocks = [b for v in one for b in (v if isinstance(v, list) else [v])]
    values = [*zero, *blocks]
    vmem = pl.BlockSpec(memory_space=pltpu.VMEM)
    return pl.pallas_call(
        functools.partial(choose_kernel, len(zero)),
        in_specs=[pl.BlockSpec(memory_space=pltpu.SMEM)] + [vmem] * len(values),
        out_specs=(vmem,) * len(zero),
        out_shape=(jax.ShapeDtypeStruct(zero[0].shape, zero[0].dtype),) * len(zero),
        compiler_params=pltpu.CompilerParams(vmem_limit_bytes=STEP_LIMIT),
        name="choose",
    )(place, *values)


def core_to_core(value, source):
    return send(value, lambda x, z, y, c: (x, z, y, 1 - c) if c == source else None)


def rows_at(dz):
    return [(dz, dy) for dy in (0, -1, 2, 1)]


def column_at(dy, zs):
    return [(dz, dy) for dz in zs]


def in_halves(source, near, wide):
    return tuple((source, False, near[n : n + 2], wide[n : n + 2]) for n in (0, 2))


def from_other(where):
    return (where[0], True, *where[2:])


Z_HEAD, Z_TAIL = (0, -1, -2, 1), (-3, 4, 2, 3)
HEAD = (None, False, rows_at(0), column_at(0, Z_HEAD))
LEAD = (None, False, rows_at(-1), column_at(-1, Z_HEAD))
LAG1 = (None, False, rows_at(1), column_at(1, Z_HEAD))
TAIL = (1, False, column_at(0, Z_TAIL), column_at(0, Z_TAIL))
LEAD2 = (None, False, rows_at(-2), column_at(-1, Z_TAIL))
LAG2 = (None, False, rows_at(2), column_at(1, Z_TAIL))
LEAD3 = (None, False, rows_at(-3), column_at(2, Z_HEAD))
LAG3 = (None, False, rows_at(3), column_at(2, Z_TAIL))
FAR = in_halves(0, rows_at(4), rows_at(4))


def item_of(tick, x):
    return jnp.clip(tick - LAG * x, 0, ITEMS - 1)


def step_kernel(tick, which, meta, consts, env, *refs):
    refs = list(refs)
    arrived = refs.pop(0) if tick >= LAG else None
    both = refs[0]
    e_out, kept, hop, *swaps, current, early = refs[-5 - len(which) :]
    x, zl = meta[0], meta[1]
    turn = tick - LAG * x
    valid = (turn >= 0) & (turn < ITEMS)
    item = item_of(tick, x)
    k, own = lax.rem(item, 4), item // 4
    sec = 2 * zl + own
    target = meta[2 + 4 * k + sec]

    if tick == 0:
        e_out[...] = jnp.zeros_like(e_out)

    @pl.when(x == 0)
    def _():
        current[...] = env[item]

    if tick >= LAG:

        @pl.when(x != 0)
        def _():
            current[...] = arrived[...]

    @pl.when(valid)
    def _():
        def two_sites(pair, carry):
            for s in (2 * pair, 2 * pair + 1):
                middle = jnp.dot(current[...], both[s, target, :, :WIDE], preferred_element_type=jnp.float32).astype(jnp.bfloat16)
                total = consts[4 * s + k] * both[s, sec, :, WIDE:].astype(jnp.float32)
                for d in range(LOCAL):
                    cols = slice(d * BLK, (d + 1) * BLK)
                    total += lax.dot_general(both[s, sec, :, cols], middle[:, cols], FIRST_AXES, preferred_element_type=jnp.float32)
                new = total.astype(jnp.bfloat16)
                current[...] = new
                e_out[own, s] += consts[16 + 4 * s + k] * new.astype(jnp.float32)

            @pl.when(pair == 0)
            def _():
                early[...] = current[...]

            return carry

        lax.fori_loop(0, 2, two_sites, 0)
        hop[...] = current[...]

        @pl.when(zl == 0)
        def _():
            kept[item] = early[...]

        @pl.when(zl == 1)
        def _():
            kept[item] = current[...]

        for part, swap in zip(which, swaps):
            first, end = PARTS[part]
            inside = (item >= first) & (item < end)

            @pl.when(inside & (zl == 0))
            def _():
                swap[item - first] = current[...]

            @pl.when(inside & (zl == 1))
            def _():
                swap[item - first] = early[...]


def parts_at(tick):
    turns = [tick - LAG * x for x in range(NX)]
    return [n for n, (first, end) in enumerate(PARTS) if any(first <= turn < end for turn in turns)]


def step(tick, meta, consts, env, arrived, both, energy, kept, swaps):
    vmem, smem = pl.BlockSpec(memory_space=pltpu.VMEM), pl.BlockSpec(memory_space=pltpu.SMEM)
    which = parts_at(tick)
    operands = [env]
    if tick >= LAG:
        operands.append(arrived)
    operands += [both]
    aliases = {}
    if tick > 0:
        aliases = {2 + len(operands): 0, 3 + len(operands): 1}
        operands += [energy, kept]
    for n, part in enumerate(which):
        if part in swaps:
            aliases[2 + len(operands)] = 3 + n
            operands.append(swaps[part])
    energy, kept, hop, *outs = pl.pallas_call(
        functools.partial(step_kernel, tick, which),
        in_specs=[smem, smem] + [vmem] * len(operands),
        out_specs=(vmem,) * (3 + len(which)),
        out_shape=(
            pltpu.VMEM((2, 4, BLK, BLK), jnp.float32),
            pltpu.VMEM((ITEMS, BLK, BLK), jnp.bfloat16),
            pltpu.VMEM((BLK, BLK), jnp.bfloat16),
        )
        + tuple(pltpu.VMEM((PARTS[n][1] - PARTS[n][0], BLK, BLK), jnp.bfloat16) for n in which),
        scratch_shapes=[pltpu.VMEM((BLK, BLK), jnp.bfloat16)] * 2,
        input_output_aliases=aliases,
        compiler_params=pltpu.CompilerParams(vmem_limit_bytes=STEP_LIMIT),
        name="renormalize",
    )(meta, consts, *[held(v) for v in operands])
    return energy, kept, hop, dict(zip(which, outs))


def place_kernel(part, meta, *refs):
    other, out, sem = refs[0], refs[-2], refs[-1]
    zl = meta[1]
    first, end = PARTS[part]
    copies = []
    for n, item in enumerate(range(first, end)):
        copies.append(pltpu.make_async_copy(other.at[n], out.at[item % 4, 2 * (1 - zl) + item // 4], sem.at[n]))
    if part == 0:
        kept = refs[1]
        for item in range(ITEMS):
            copies.append(pltpu.make_async_copy(kept.at[item], out.at[item % 4, 2 * zl + item // 4], sem.at[ITEMS + item]))
    for copy in copies:
        copy.start()
    for copy in copies:
        copy.wait()


def place_items(part, meta, other, rest):
    vmem, hbm = pl.BlockSpec(memory_space=pltpu.VMEM), pl.BlockSpec(memory_space=pltpu.HBM)
    return pl.pallas_call(
        functools.partial(place_kernel, part),
        in_specs=[pl.BlockSpec(memory_space=pltpu.SMEM), vmem, vmem if part == 0 else hbm],
        out_specs=hbm,
        out_shape=pltpu.HBM((4, SECT, BLK, BLK), jnp.bfloat16),
        scratch_shapes=[pltpu.SemaphoreType.DMA((2 * ITEMS,))],
        input_output_aliases={} if part == 0 else {2: 0},
        compiler_params=pltpu.CompilerParams(vmem_limit_bytes=STEP_LIMIT),
        name="place_items",
    )(meta, other, rest)


def piece(value, axis, place, size):
    return lax.dynamic_slice_in_dim(value, place * size, size, axis)


def on_core(body, place, operands, shapes, out_hbm=False):
    vmem = pl.BlockSpec(memory_space=pltpu.VMEM)
    return pl.pallas_call(
        body,
        in_specs=[pl.BlockSpec(memory_space=pltpu.SMEM)] + [vmem] * len(operands),
        out_specs=(vmem,) * len(shapes),
        out_shape=tuple(jax.ShapeDtypeStruct(shape, dtype) for shape, dtype in shapes),
        compiler_params=pltpu.CompilerParams(vmem_limit_bytes=2 * STEP_LIMIT),
        name=body.__name__,
    )(place, *operands)


HALF, QUARTER = BLK // 2, BLK // 8
AROUND = (2, 1, -1)
ALONG = (4, 3, -3, 2, -2, 1, -1)


def rows_of(place, count):
    return pl.ds(pl.multiple_of(place * count, count), count)


def halve(place, energy, out):
    out[...] = energy[:, :, rows_of(1 - place[2], HALF), :].astype(jnp.bfloat16)


def quarter(place, energy, got, own, *outs):
    own_rows, y = rows_of(place[2], HALF), place[1]

    def total(at):
        first = pl.multiple_of(place[2] * HALF + at * QUARTER, QUARTER)
        return energy[:, :, pl.ds(first, QUARTER), :] + got[:, :, rows_of(at, QUARTER), :].astype(jnp.float32)

    own[...] = total(y)
    for out, step in zip(outs, AROUND):
        out[...] = total(lax.rem(y + NY + step, NY)).astype(jnp.bfloat16)


def by_lane(place, own, first, second, third, mine, near, far):
    zl = place[3]

    def total(lane):
        at = pl.ds(2 * lane, 2)
        return own[:, at] + (first[:, at].astype(jnp.float32) + second[:, at].astype(jnp.float32) + third[:, at].astype(jnp.float32))

    mine[...] = total(zl)
    near[...] = mine[...].astype(jnp.bfloat16)
    far[...] = total(1 - zl).astype(jnp.bfloat16)


def line_up(place, mine, *refs):
    out, zl = refs[-1], place[3]

    def total(parity):
        return sum(ref[...].astype(jnp.float32) for ref, step in zip(refs, ALONG) if step % 2 == parity)

    same, other = mine[...] + total(0), total(1)
    for n in range(2):
        for sector in range(2):
            out[n, 2 * zl + sector] = same[sector, n].astype(jnp.bfloat16)
            out[n, 2 * (1 - zl) + sector] = other[sector, n].astype(jnp.bfloat16)


def join_y(place, own, first, second, third, out):
    out[:, :, rows_of(place[1], QUARTER), :] = own[...]
    for ref, step in zip((first, second, third), AROUND):
        out[:, :, rows_of(lax.rem(place[1] + NY - step, NY), QUARTER), :] = ref[...]


def join_core(place, own, other, out):
    out[:, :, rows_of(place[2], HALF), :] = own[...].astype(jnp.float32)
    out[:, :, rows_of(1 - place[2], HALF), :] = other[...].astype(jnp.float32)


def reduce_energy(energy, place, meta, kept, ended):
    bf16, f32 = jnp.bfloat16, jnp.float32
    energy = held(energy)
    (theirs,) = on_core(halve, place, [energy], [((2, 4, HALF, BLK), bf16)])
    got = other_core(theirs)
    shape = (2, 4, QUARTER, BLK)
    own, *parts = on_core(quarter, place, [energy, got], [(shape, f32)] + [(shape, bf16)] * 3)
    parts = [along_y(part, step) for part, step in zip(parts, AROUND)]
    shape = (2, 2, QUARTER, BLK)
    mine, near, far = on_core(by_lane, place, [own, *parts], [(shape, f32)] + [(shape, bf16)] * 2)
    parts = [along_z(far if step % 2 else near, step) for step in ALONG]
    out = place_items(0, meta, other_lane(ended[0]), kept)
    parts, late, out = lax.optimization_barrier((parts, ended[1], out))
    late = other_lane(late)
    (flat,) = on_core(line_up, place, [mine, *parts], [((2, 4, QUARTER, BLK), bf16)])
    parts = [along_y(flat, step) for step in AROUND]
    parts[-1], late = lax.optimization_barrier((parts[-1], late))
    out = place_items(1, meta, late, out)
    (flat,) = on_core(join_y, place, [flat, *parts], [((2, 4, HALF, BLK), bf16)])
    (flat,) = on_core(join_core, place, [flat, other_core(flat)], [((2, 4, BLK, BLK), f32)])
    return out[None], flat


def pick_kernel(pair_of, coupling, weight, out):
    for s in range(2):
        for k in range(4):
            out[4 * s + k] = coupling[s, pair_of[k]]
            out[8 + 4 * s + k] = weight[s, pair_of[k]]


def pick(pair_of, coupling, weight):
    smem = pl.BlockSpec(memory_space=pltpu.SMEM)
    return pl.pallas_call(
        pick_kernel,
        in_specs=[smem] * 3,
        out_specs=smem,
        out_shape=jax.ShapeDtypeStruct((16,), jnp.float32),
        name="pick",
    )(pair_of, coupling, weight)


def local(environment, rotations, site_terms, pair_of, targets, coupling, energy_coef):
    sweep, op = lax.axis_index("sweep"), lax.axis_index("op")
    x, zl = sweep // 2, sweep % 2
    zh, y, c = op // 8, (op // 2) % 4, op % 2
    z = 2 * zh + zl

    wide = jnp.concatenate([rotations, site_terms], axis=3)
    mine, theirs = wide[c], wide[1 - c]
    got = other_core(theirs)
    block = jnp.where(c == 0, jnp.concatenate([mine, got], axis=1), jnp.concatenate([got, mine], axis=1))
    place = jnp.stack([z, y, c, zl]).astype(jnp.int32)

    def prepare(operands):
        pair_of, targets, coupling, energy_coef, environment = operands
        values = pick(pair_of, coupling, energy_coef).reshape(2, 8)
        got = other_lane(values)
        consts = jnp.where(zl == 0, jnp.concatenate([values, got], axis=1), jnp.concatenate([got, values], axis=1)).reshape(-1)
        meta = jnp.concatenate([jnp.stack([x, zl]).astype(jnp.int32), targets.reshape(-1)])
        env = piece(environment, 1, zl, 2).swapaxes(0, 1).reshape(ITEMS, BLK, BLK)
        return consts, meta, env

    operands = (pair_of, targets, coupling, energy_coef, environment)
    both, (consts, meta, env) = gather_plane(block, place, operands, prepare)

    energy, kept, swaps, hops, ended = None, None, {}, [], {}
    for tick in range(TICKS):
        arrived = hops[tick - LAG] if tick >= LAG else None
        energy, kept, hop, swaps = step(tick, meta, consts, env, arrived, both, energy, kept, swaps)
        hops.append(next_stage(hop) if tick < TICKS - LAG else None)
        for part in swaps:
            if part not in parts_at(tick + 1):
                ended[part] = swaps[part]
    return reduce_energy(energy, place, meta, kept, ended)


def solution(mesh):
    return jax.shard_map(
        local,
        mesh=mesh,
        in_specs=(
            P("op", None, None, None),
            P("sweep", None, "op", None),
            P("sweep", None, "op", None),
            P("op"),
            P("op", None),
            P("sweep", None),
            P("sweep", None),
        ),
        out_specs=(P("sweep", "op", None, None, None), P("sweep", None, None, None)),
        check_vma=False,
    )
```

```python
import functools

import jax
import jax.numpy as jnp
from jax import lax
from jax.experimental import pallas as pl
from jax.experimental.pallas import tpu as pltpu
from jax.sharding import PartitionSpec as P

NX, NZL, NZH, NY, NC = 4, 2, 4, 4, 2
NZ = NZL * NZH
SECT, BLK, LOCAL = 4, 256, 4
WIDE = LOCAL * BLK
BOTH = WIDE + BLK
ITEMS = 8
SPLIT = 4
PARTS = ((0, SPLIT), (SPLIT, ITEMS))
LAG = 2
TICKS = ITEMS + LAG * (NX - 1)
STEP_LIMIT = 8 * 1024 * 1024

FIRST_AXES = (((0,), (0,)), ((), ()))
AXES = ("sweep", "op")


def number(x, z, y, c):
    zh, zl = z // 2, z % 2
    return (x * NZL + zl) * (NZH * NY * NC) + (zh * NY + y) * NC + c


def send(value, rule):
    pairs = []
    for x in range(NX):
        for z in range(NZ):
            for y in range(NY):
                for c in range(NC):
                    to = rule(x, z, y, c)
                    if to is not None:
                        pairs.append((number(x, z, y, c), number(*to)))
    return lax.ppermute(value, AXES, pairs)


def along_y(value, step):
    return send(value, lambda x, z, y, c: (x, z, (y + step) % NY, c))


def along_z(value, step):
    return send(value, lambda x, z, y, c: (x, (z + step) % NZ, y, c))


def other_core(value):
    return send(value, lambda x, z, y, c: (x, z, y, 1 - c))


def other_lane(value):
    return send(value, lambda x, z, y, c: (x, z ^ 1, y, c))


def next_stage(value):
    return send(value, lambda x, z, y, c: (x + 1, z, y, c) if x + 1 < NX else None)


def after(value, *others):
    return lax.optimization_barrier((value, others))[0]


def held(value):
    return pltpu.with_memory_space_constraint(value, pltpu.VMEM)


def put_kernel(layout, place, *refs):
    both, sem = refs[-2:]
    z, y, c = place[0], place[1], place[2]
    copies = []
    for n, (ref, (source, other, near, wide)) in enumerate(zip(refs, layout)):
        core = 1 - c if other else c
        does = None if source is None else core == source
        for lead, (p, q) in enumerate(zip(near, wide)):
            zs = lax.rem(z + NZ + jnp.where(core == 0, p[0], q[0]), NZ)
            ys = lax.rem(y + NY + jnp.where(core == 0, p[1], q[1]), NY)
            row = pl.ds(pl.multiple_of(((zs // 2) * NY + ys) * 16, 16), 16)
            to = both.at[2 * lax.rem(zs, 2) + core, :, row, :]
            copies.append((does, pltpu.make_async_copy(ref.at[lead], to, sem.at[n, lead])))
    for does, copy in copies:
        if does is None:
            copy.start()
        else:
            pl.when(does)(copy.start)
    for does, copy in copies:
        if does is None:
            copy.wait()
        else:
            pl.when(does)(copy.wait)


def put(place, pieces, into):
    layout = [where for _, where in pieces]
    values = [value for value, _ in pieces]
    count = len(pieces)
    vmem, anywhere = pl.BlockSpec(memory_space=pltpu.VMEM), pl.BlockSpec(memory_space=pl.ANY)
    extra = [] if into is None else [held(into)]
    return pl.pallas_call(
        functools.partial(put_kernel, layout),
        out_shape=pltpu.VMEM((4, SECT, BLK, BOTH), jnp.bfloat16),
        in_specs=[pl.BlockSpec(memory_space=pltpu.SMEM)] + [anywhere] * count + [vmem] * len(extra),
        out_specs=vmem,
        scratch_shapes=[pltpu.SemaphoreType.DMA((count, 4))],
        input_output_aliases={} if into is None else {1 + count: 0},
        compiler_params=pltpu.CompilerParams(vmem_limit_bytes=STEP_LIMIT),
        name="put",
    )(place, *values, *extra)


def by_core(value, near, wide):
    def rule(x, z, y, c):
        move = near if c == 0 else wide
        if move is None:
            return None
        return x, (z + move[0]) % NZ, (y + move[1]) % NY, c

    return send(value, rule)


def gather_plane(block, place, extra, prepare):
    together = lax.optimization_barrier
    up, down, right, left = (1, 0), (-1, 0), (0, 1), (0, -1)
    up2, down2, right2 = (2, 0), (-2, 0), (0, 2)
    right2, up2, down2 = (0, 2), (2, 0), (-2, 0)
    near = [by_core(block, right, up), by_core(block, left, down), by_core(block, right2, up2), by_core(block, None, down2)]
    lower, upper, lower2, upper2 = together(tuple(near))
    head = jnp.stack([block, lower, lower2, upper])

    lower3, lower4, upper3 = by_core(lower, None, up2), by_core(lower2, None, up2), by_core(upper, None, down2)
    lead, lag = by_core(head, up, right), by_core(head, down, left)
    lead, lag, lower3, lower4, upper3 = together((lead, lag, lower3, lower4, upper3))
    third, fourth = choose(place, [lead, lag], [[lower3, lower4, upper2, upper3]] * 2)
    third, fourth, extra, head, lead, lag = together((third, fourth, extra, head, lead, lag))

    lead2, lag2 = by_core(third, up, right), by_core(fourth, down, left)
    extra = prepare(extra)
    ready = [(head, HEAD), (lead, LEAD), (lag, LAG1)]
    ready += [(other_core(v), from_other(w)) for v, w in ready]
    ready += [(third, TAIL), (core_to_core(third, 1), from_other(TAIL))]
    lead2, lag2, extra = together((lead2, lag2, extra))
    up_halves, down_halves = choose(place, [lead2, lag2], [lead, lag2], True)

    lead3 = [by_core(half, up, right) for half in up_halves]
    lag3 = [by_core(half, down, left) for half in down_halves]
    into = put(place, ready, None)
    lead3, lag3, lead2, lag2, into = together((lead3, lag3, lead2, lag2, into))

    far = by_core(lead3[0], up, None), by_core(lag3[1], down, None)
    ready = [(lead2, LEAD2), (lag2, LAG2)]
    into = put(place, ready + [(other_core(v), from_other(w)) for v, w in ready], into)
    ready = [(v, w) for v, w in zip([*lead3, *lag3], LEAD3 + LAG3)]
    ready += [(other_core(v), from_other(w)) for v, w in ready]
    far, into = together((far, into))
    for v, w in zip(far, FAR):
        ready += [(v, w), (core_to_core(v, 0), from_other(w))]
    return put(place, ready, into), extra


def choose_kernel(parts, place, *refs):
    values, outs = refs[:-parts], refs[-parts:]
    half = parts // 2
    rest = (len(values) - 2) // 2

    def fill(n, sources):
        for m in range(4):
            out = outs[n * half + (m // 2 if half == 2 else 0)]
            at = m % 2 if half == 2 else m
            out[at] = sources[0][m] if len(sources) == 1 else sources[m][...]

    for n in range(2):
        pl.when(place[2] == 0)(functools.partial(fill, n, values[n : n + 1]))
        pl.when(place[2] == 1)(functools.partial(fill, n, values[2 + n * rest : 2 + (n + 1) * rest]))


def choose(place, zero, one, in_two=False):
    one = [v if isinstance(v, list) else [v] for v in one]
    values = [*zero, *one[0], *one[1]]
    parts = 4 if in_two else 2
    shape = (2 if in_two else 4, *zero[0].shape[1:])
    vmem = pl.BlockSpec(memory_space=pltpu.VMEM)
    outs = pl.pallas_call(
        functools.partial(choose_kernel, parts),
        in_specs=[pl.BlockSpec(memory_space=pltpu.SMEM)] + [vmem] * len(values),
        out_specs=(vmem,) * parts,
        out_shape=(jax.ShapeDtypeStruct(shape, zero[0].dtype),) * parts,
        compiler_params=pltpu.CompilerParams(vmem_limit_bytes=STEP_LIMIT),
        name="choose",
    )(place, *values)
    return (outs[:2], outs[2:]) if in_two else outs


def core_to_core(value, source):
    return send(value, lambda x, z, y, c: (x, z, y, 1 - c) if c == source else None)


def rows_at(dz):
    return [(dz, dy) for dy in (0, -1, 2, 1)]


def column_at(dy, zs):
    return [(dz, dy) for dz in zs]


def in_halves(source, near, wide):
    return tuple((source, False, near[n : n + 2], wide[n : n + 2]) for n in (0, 2))


def from_other(where):
    return (where[0], True, *where[2:])


Z_HEAD, Z_TAIL = (0, -1, -2, 1), (-3, 4, 2, 3)
HEAD = (None, False, rows_at(0), column_at(0, Z_HEAD))
LEAD = (None, False, rows_at(-1), column_at(-1, Z_HEAD))
LAG1 = (None, False, rows_at(1), column_at(1, Z_HEAD))
TAIL = (1, False, column_at(0, Z_TAIL), column_at(0, Z_TAIL))
LEAD2 = (None, False, rows_at(-2), column_at(-1, Z_TAIL))
LAG2 = (None, False, rows_at(2), column_at(1, Z_TAIL))
LEAD3 = in_halves(None, rows_at(-3), column_at(2, Z_HEAD))
LAG3 = in_halves(None, rows_at(3), column_at(2, Z_TAIL))
FAR = in_halves(0, rows_at(4), rows_at(4))


def item_of(tick, x):
    return jnp.clip(tick - LAG * x, 0, ITEMS - 1)


def step_kernel(tick, which, meta, consts, env, *refs):
    refs = list(refs)
    arrived = refs.pop(0) if tick >= LAG else None
    both = refs[0]
    e_out, kept, hop, *swaps, current, early = refs[-5 - len(which) :]
    x, zl = meta[0], meta[1]
    turn = tick - LAG * x
    valid = (turn >= 0) & (turn < ITEMS)
    item = item_of(tick, x)
    k, own = lax.rem(item, 4), item // 4
    sec = 2 * zl + own
    target = meta[2 + 4 * k + sec]

    if tick == 0:
        e_out[...] = jnp.zeros_like(e_out)

    @pl.when(x == 0)
    def _():
        current[...] = env[item]

    if tick >= LAG:

        @pl.when(x != 0)
        def _():
            current[...] = arrived[...]

    @pl.when(valid)
    def _():
        for s in range(4):
            middle = jnp.dot(current[...], both[s, target, :, :WIDE], preferred_element_type=jnp.float32).astype(jnp.bfloat16)
            total = consts[4 * s + k] * both[s, sec, :, WIDE:].astype(jnp.float32)
            for d in range(LOCAL):
                cols = slice(d * BLK, (d + 1) * BLK)
                total += lax.dot_general(both[s, sec, :, cols], middle[:, cols], FIRST_AXES, preferred_element_type=jnp.float32)
            new = total.astype(jnp.bfloat16)
            current[...] = new
            if s == 1:
                early[...] = new
            if s == 3:
                hop[...] = new
            e_out[own, s] += consts[16 + 4 * s + k] * new.astype(jnp.float32)

        @pl.when(zl == 0)
        def _():
            kept[item] = early[...]

        @pl.when(zl == 1)
        def _():
            kept[item] = current[...]

        for part, swap in zip(which, swaps):
            first, end = PARTS[part]
            inside = (item >= first) & (item < end)

            @pl.when(inside & (zl == 0))
            def _():
                swap[item - first] = current[...]

            @pl.when(inside & (zl == 1))
            def _():
                swap[item - first] = early[...]


def parts_at(tick):
    turns = [tick - LAG * x for x in range(NX)]
    return [n for n, (first, end) in enumerate(PARTS) if any(first <= turn < end for turn in turns)]


def step(tick, meta, consts, env, arrived, both, energy, kept, swaps):
    vmem, smem = pl.BlockSpec(memory_space=pltpu.VMEM), pl.BlockSpec(memory_space=pltpu.SMEM)
    which = parts_at(tick)
    operands = [env]
    if tick >= LAG:
        operands.append(arrived)
    operands += [both]
    aliases = {}
    if tick > 0:
        aliases = {2 + len(operands): 0, 3 + len(operands): 1}
        operands += [energy, kept]
    for n, part in enumerate(which):
        if part in swaps:
            aliases[2 + len(operands)] = 3 + n
            operands.append(swaps[part])
    energy, kept, hop, *outs = pl.pallas_call(
        functools.partial(step_kernel, tick, which),
        in_specs=[smem, smem] + [vmem] * len(operands),
        out_specs=(vmem,) * (3 + len(which)),
        out_shape=(
            pltpu.VMEM((2, 4, BLK, BLK), jnp.float32),
            pltpu.VMEM((ITEMS, BLK, BLK), jnp.bfloat16),
            pltpu.VMEM((BLK, BLK), jnp.bfloat16),
        )
        + tuple(pltpu.VMEM((PARTS[n][1] - PARTS[n][0], BLK, BLK), jnp.bfloat16) for n in which),
        scratch_shapes=[pltpu.VMEM((BLK, BLK), jnp.bfloat16)] * 2,
        input_output_aliases=aliases,
        compiler_params=pltpu.CompilerParams(vmem_limit_bytes=STEP_LIMIT),
        name="renormalize",
    )(meta, consts, *[held(v) for v in operands])
    return energy, kept, hop, dict(zip(which, outs))


def place_kernel(part, meta, *refs):
    other, out, sem = refs[0], refs[-2], refs[-1]
    zl = meta[1]
    first, end = PARTS[part]
    copies = []
    for n, item in enumerate(range(first, end)):
        copies.append(pltpu.make_async_copy(other.at[n], out.at[item % 4, 2 * (1 - zl) + item // 4], sem.at[n]))
    if part == 0:
        kept = refs[1]
        for item in range(ITEMS):
            copies.append(pltpu.make_async_copy(kept.at[item], out.at[item % 4, 2 * zl + item // 4], sem.at[ITEMS + item]))
    for copy in copies:
        copy.start()
    for copy in copies:
        copy.wait()


def place_items(part, meta, other, rest):
    vmem, hbm = pl.BlockSpec(memory_space=pltpu.VMEM), pl.BlockSpec(memory_space=pltpu.HBM)
    return pl.pallas_call(
        functools.partial(place_kernel, part),
        in_specs=[pl.BlockSpec(memory_space=pltpu.SMEM), vmem, vmem if part == 0 else hbm],
        out_specs=hbm,
        out_shape=pltpu.HBM((4, SECT, BLK, BLK), jnp.bfloat16),
        scratch_shapes=[pltpu.SemaphoreType.DMA((2 * ITEMS,))],
        input_output_aliases={} if part == 0 else {2: 0},
        compiler_params=pltpu.CompilerParams(vmem_limit_bytes=STEP_LIMIT),
        name="place_items",
    )(meta, other, rest)


def piece(value, axis, place, size):
    return lax.dynamic_slice_in_dim(value, place * size, size, axis)


def on_core(body, place, operands, shapes, out_hbm=False):
    vmem = pl.BlockSpec(memory_space=pltpu.VMEM)
    return pl.pallas_call(
        body,
        in_specs=[pl.BlockSpec(memory_space=pltpu.SMEM)] + [vmem] * len(operands),
        out_specs=(vmem,) * len(shapes),
        out_shape=tuple(jax.ShapeDtypeStruct(shape, dtype) for shape, dtype in shapes),
        compiler_params=pltpu.CompilerParams(vmem_limit_bytes=2 * STEP_LIMIT),
        name=body.__name__,
    )(place, *operands)


HALF, QUARTER = BLK // 2, BLK // 8
AROUND = (2, 1, -1)
ALONG = (4, 3, -3, 2, -2, 1, -1)


def rows_of(place, count):
    return pl.ds(pl.multiple_of(place * count, count), count)


def halve(place, energy, out):
    out[...] = energy[:, :, rows_of(1 - place[2], HALF), :].astype(jnp.bfloat16)


def quarter(place, energy, got, own, *outs):
    own_rows, y = rows_of(place[2], HALF), place[1]

    def total(at):
        first = pl.multiple_of(place[2] * HALF + at * QUARTER, QUARTER)
        return energy[:, :, pl.ds(first, QUARTER), :] + got[:, :, rows_of(at, QUARTER), :].astype(jnp.float32)

    own[...] = total(y)
    for out, step in zip(outs, AROUND):
        out[...] = total(lax.rem(y + NY + step, NY)).astype(jnp.bfloat16)


def by_lane(place, own, first, second, third, mine, near, far):
    zl = place[3]

    def total(lane):
        at = pl.ds(2 * lane, 2)
        return own[:, at] + (first[:, at].astype(jnp.float32) + second[:, at].astype(jnp.float32) + third[:, at].astype(jnp.float32))

    mine[...] = total(zl)
    near[...] = mine[...].astype(jnp.bfloat16)
    far[...] = total(1 - zl).astype(jnp.bfloat16)


def line_up(place, mine, *refs):
    out, zl = refs[-1], place[3]

    def total(parity):
        return sum(ref[...].astype(jnp.float32) for ref, step in zip(refs, ALONG) if step % 2 == parity)

    same, other = mine[...] + total(0), total(1)
    for n in range(2):
        for sector in range(2):
            out[n, 2 * zl + sector] = same[sector, n].astype(jnp.bfloat16)
            out[n, 2 * (1 - zl) + sector] = other[sector, n].astype(jnp.bfloat16)


def join_y(place, own, first, second, third, out):
    out[:, :, rows_of(place[1], QUARTER), :] = own[...]
    for ref, step in zip((first, second, third), AROUND):
        out[:, :, rows_of(lax.rem(place[1] + NY - step, NY), QUARTER), :] = ref[...]


def join_core(place, own, other, out):
    out[:, :, rows_of(place[2], HALF), :] = own[...].astype(jnp.float32)
    out[:, :, rows_of(1 - place[2], HALF), :] = other[...].astype(jnp.float32)


def reduce_energy(energy, place, meta, kept, ended):
    bf16, f32 = jnp.bfloat16, jnp.float32
    energy = held(energy)
    (theirs,) = on_core(halve, place, [energy], [((2, 4, HALF, BLK), bf16)])
    got = other_core(theirs)
    shape = (2, 4, QUARTER, BLK)
    own, *parts = on_core(quarter, place, [energy, got], [(shape, f32)] + [(shape, bf16)] * 3)
    parts = [along_y(part, step) for part, step in zip(parts, AROUND)]
    shape = (2, 2, QUARTER, BLK)
    mine, near, far = on_core(by_lane, place, [own, *parts], [(shape, f32)] + [(shape, bf16)] * 2)
    parts = [along_z(far if step % 2 else near, step) for step in ALONG]
    out = place_items(0, meta, other_lane(ended[0]), kept)
    parts, late, out = lax.optimization_barrier((parts, ended[1], out))
    late = other_lane(late)
    (flat,) = on_core(line_up, place, [mine, *parts], [((2, 4, QUARTER, BLK), bf16)])
    parts = [along_y(flat, step) for step in AROUND]
    parts[-1], late = lax.optimization_barrier((parts[-1], late))
    out = place_items(1, meta, late, out)
    (flat,) = on_core(join_y, place, [flat, *parts], [((2, 4, HALF, BLK), bf16)])
    (flat,) = on_core(join_core, place, [flat, other_core(flat)], [((2, 4, BLK, BLK), f32)])
    return out[None], flat


def pick_kernel(pair_of, coupling, weight, out):
    for s in range(2):
        for k in range(4):
            out[4 * s + k] = coupling[s, pair_of[k]]
            out[8 + 4 * s + k] = weight[s, pair_of[k]]


def pick(pair_of, coupling, weight):
    smem = pl.BlockSpec(memory_space=pltpu.SMEM)
    return pl.pallas_call(
        pick_kernel,
        in_specs=[smem] * 3,
        out_specs=smem,
        out_shape=jax.ShapeDtypeStruct((16,), jnp.float32),
        name="pick",
    )(pair_of, coupling, weight)


def local(environment, rotations, site_terms, pair_of, targets, coupling, energy_coef):
    sweep, op = lax.axis_index("sweep"), lax.axis_index("op")
    x, zl = sweep // 2, sweep % 2
    zh, y, c = op // 8, (op // 2) % 4, op % 2
    z = 2 * zh + zl

    wide = jnp.concatenate([rotations, site_terms], axis=3)
    mine, theirs = wide[c], wide[1 - c]
    got = other_core(theirs)
    block = jnp.where(c == 0, jnp.concatenate([mine, got], axis=1), jnp.concatenate([got, mine], axis=1))
    place = jnp.stack([z, y, c, zl]).astype(jnp.int32)

    def prepare(operands):
        pair_of, targets, coupling, energy_coef, environment = operands
        values = pick(pair_of, coupling, energy_coef).reshape(2, 8)
        got = other_lane(values)
        consts = jnp.where(zl == 0, jnp.concatenate([values, got], axis=1), jnp.concatenate([got, values], axis=1)).reshape(-1)
        meta = jnp.concatenate([jnp.stack([x, zl]).astype(jnp.int32), targets.reshape(-1)])
        env = piece(environment, 1, zl, 2).swapaxes(0, 1).reshape(ITEMS, BLK, BLK)
        return consts, meta, env

    operands = (pair_of, targets, coupling, energy_coef, environment)
    both, (consts, meta, env) = gather_plane(block, place, operands, prepare)

    energy, kept, swaps, hops, ended = None, None, {}, [], {}
    for tick in range(TICKS):
        arrived = hops[tick - LAG] if tick >= LAG else None
        energy, kept, hop, swaps = step(tick, meta, consts, env, arrived, both, energy, kept, swaps)
        hops.append(next_stage(hop) if tick < TICKS - LAG else None)
        for part in swaps:
            if part not in parts_at(tick + 1):
                ended[part] = swaps[part]
    return reduce_energy(energy, place, meta, kept, ended)


def solution(mesh):
    return jax.shard_map(
        local,
        mesh=mesh,
        in_specs=(
            P("op", None, None, None),
            P("sweep", None, "op", None),
            P("sweep", None, "op", None),
            P("op"),
            P("op", None),
            P("sweep", None),
            P("sweep", None),
        ),
        out_specs=(P("sweep", "op", None, None, None), P("sweep", None, None, None)),
        check_vma=False,
    )
```

```python
import functools

import jax
import jax.numpy as jnp
from jax import lax
from jax.experimental import pallas as pl
from jax.experimental.pallas import tpu as pltpu
from jax.sharding import PartitionSpec as P

NX, NZL, NZH, NY, NC = 4, 2, 4, 4, 2
NZ = NZL * NZH
SECT, BLK, LOCAL = 4, 256, 4
WIDE = LOCAL * BLK
BOTH = WIDE + BLK
ITEMS = 8
SPLIT = 4
PARTS = ((0, SPLIT), (SPLIT, ITEMS))
LAG = 2
TICKS = ITEMS + LAG * (NX - 1)
STEP_LIMIT = 8 * 1024 * 1024

FIRST_AXES = (((0,), (0,)), ((), ()))
AXES = ("sweep", "op")


def number(x, z, y, c):
    zh, zl = z // 2, z % 2
    return (x * NZL + zl) * (NZH * NY * NC) + (zh * NY + y) * NC + c


def send(value, rule):
    pairs = []
    for x in range(NX):
        for z in range(NZ):
            for y in range(NY):
                for c in range(NC):
                    to = rule(x, z, y, c)
                    if to is not None:
                        pairs.append((number(x, z, y, c), number(*to)))
    return lax.ppermute(value, AXES, pairs)


def along_y(value, step):
    return send(value, lambda x, z, y, c: (x, z, (y + step) % NY, c))


def along_z(value, step):
    return send(value, lambda x, z, y, c: (x, (z + step) % NZ, y, c))


def other_core(value):
    return send(value, lambda x, z, y, c: (x, z, y, 1 - c))


def other_lane(value):
    return send(value, lambda x, z, y, c: (x, z ^ 1, y, c))


def next_stage(value):
    return send(value, lambda x, z, y, c: (x + 1, z, y, c) if x + 1 < NX else None)


def after(value, *others):
    return lax.optimization_barrier((value, others))[0]


def held(value):
    return pltpu.with_memory_space_constraint(value, pltpu.VMEM)


def put_kernel(layout, place, *refs):
    both, sem = refs[-2:]
    z, y, c = place[0], place[1], place[2]
    copies = []
    for n, (ref, (source, other, near, wide)) in enumerate(zip(refs, layout)):
        core = 1 - c if other else c
        does = None if source is None else core == source
        for lead, (p, q) in enumerate(zip(near, wide)):
            zs = lax.rem(z + NZ + jnp.where(core == 0, p[0], q[0]), NZ)
            ys = lax.rem(y + NY + jnp.where(core == 0, p[1], q[1]), NY)
            row = pl.ds(pl.multiple_of(((zs // 2) * NY + ys) * 16, 16), 16)
            to = both.at[2 * lax.rem(zs, 2) + core, :, row, :]
            copies.append((does, pltpu.make_async_copy(ref.at[lead], to, sem.at[n, lead])))
    for does, copy in copies:
        if does is None:
            copy.start()
        else:
            pl.when(does)(copy.start)
    for does, copy in copies:
        if does is None:
            copy.wait()
        else:
            pl.when(does)(copy.wait)


def put(place, pieces, into):
    layout = [where for _, where in pieces]
    values = [value for value, _ in pieces]
    count = len(pieces)
    vmem, anywhere = pl.BlockSpec(memory_space=pltpu.VMEM), pl.BlockSpec(memory_space=pl.ANY)
    extra = [] if into is None else [held(into)]
    return pl.pallas_call(
        functools.partial(put_kernel, layout),
        out_shape=pltpu.VMEM((4, SECT, BLK, BOTH), jnp.bfloat16),
        in_specs=[pl.BlockSpec(memory_space=pltpu.SMEM)] + [anywhere] * count + [vmem] * len(extra),
        out_specs=vmem,
        scratch_shapes=[pltpu.SemaphoreType.DMA((count, 4))],
        input_output_aliases={} if into is None else {1 + count: 0},
        compiler_params=pltpu.CompilerParams(vmem_limit_bytes=STEP_LIMIT),
        name="put",
    )(place, *values, *extra)


def by_core(value, near, wide):
    def rule(x, z, y, c):
        move = near if c == 0 else wide
        if move is None:
            return None
        return x, (z + move[0]) % NZ, (y + move[1]) % NY, c

    return send(value, rule)


def gather_plane(block, place, extra, prepare):
    together = lax.optimization_barrier
    up, down, right, left = (1, 0), (-1, 0), (0, 1), (0, -1)
    up2, down2, right2 = (2, 0), (-2, 0), (0, 2)
    right2, up2, down2 = (0, 2), (2, 0), (-2, 0)
    near = [by_core(block, right, up), by_core(block, left, down), by_core(block, right2, up2), by_core(block, None, down2)]
    lower, upper, lower2, upper2 = together(tuple(near))
    head = jnp.stack([block, lower, lower2, upper])

    lower3, lower4, upper3 = by_core(lower, None, up2), by_core(lower2, None, up2), by_core(upper, None, down2)
    lead, lag = by_core(head, up, right), by_core(head, down, left)
    lead, lag, lower3, lower4, upper3 = together((lead, lag, lower3, lower4, upper3))
    third, fourth = choose(place, [lead, lag], [[lower3, lower4, upper2, upper3]] * 2)
    third, fourth, extra, head, lead, lag = together((third, fourth, extra, head, lead, lag))

    lead2, lag2 = by_core(third, up, right), by_core(fourth, down, left)
    extra = prepare(extra)
    ready = [(head, HEAD), (lead, LEAD), (lag, LAG1)]
    ready += [(other_core(v), from_other(w)) for v, w in ready]
    ready += [(third, TAIL), (core_to_core(third, 1), from_other(TAIL))]
    lead2, lag2, extra = together((lead2, lag2, extra))
    up_halves, down_halves = choose(place, [lead2, lag2], [lead, lag2], True)

    lead3 = [by_core(half, up, right) for half in up_halves]
    lag3 = [by_core(half, down, left) for half in down_halves]
    into = put(place, ready, None)
    lead3, lag3, lead2, lag2, into = together((lead3, lag3, lead2, lag2, into))

    far = by_core(lead3[0], up, None), by_core(lag3[1], down, None)
    ready = [(lead2, LEAD2), (lag2, LAG2)]
    into = put(place, ready + [(other_core(v), from_other(w)) for v, w in ready], into)
    ready = [(v, w) for v, w in zip([*lead3, *lag3], LEAD3 + LAG3)]
    ready += [(other_core(v), from_other(w)) for v, w in ready]
    far, into = together((far, into))
    for v, w in zip(far, FAR):
        ready += [(v, w), (core_to_core(v, 0), from_other(w))]
    return put(place, ready, into), extra


def choose_kernel(parts, place, *refs):
    values, outs = refs[:-parts], refs[-parts:]
    half = parts // 2
    rest = (len(values) - 2) // 2

    def fill(n, sources):
        for m in range(4):
            out = outs[n * half + (m // 2 if half == 2 else 0)]
            at = m % 2 if half == 2 else m
            out[at] = sources[0][m] if len(sources) == 1 else sources[m][...]

    for n in range(2):
        pl.when(place[2] == 0)(functools.partial(fill, n, values[n : n + 1]))
        pl.when(place[2] == 1)(functools.partial(fill, n, values[2 + n * rest : 2 + (n + 1) * rest]))


def choose(place, zero, one, in_two=False):
    one = [v if isinstance(v, list) else [v] for v in one]
    values = [*zero, *one[0], *one[1]]
    parts = 4 if in_two else 2
    shape = (2 if in_two else 4, *zero[0].shape[1:])
    vmem = pl.BlockSpec(memory_space=pltpu.VMEM)
    outs = pl.pallas_call(
        functools.partial(choose_kernel, parts),
        in_specs=[pl.BlockSpec(memory_space=pltpu.SMEM)] + [vmem] * len(values),
        out_specs=(vmem,) * parts,
        out_shape=(jax.ShapeDtypeStruct(shape, zero[0].dtype),) * parts,
        compiler_params=pltpu.CompilerParams(vmem_limit_bytes=STEP_LIMIT),
        name="choose",
    )(place, *values)
    return (outs[:2], outs[2:]) if in_two else outs


def core_to_core(value, source):
    return send(value, lambda x, z, y, c: (x, z, y, 1 - c) if c == source else None)


def rows_at(dz):
    return [(dz, dy) for dy in (0, -1, 2, 1)]


def column_at(dy, zs):
    return [(dz, dy) for dz in zs]


def in_halves(source, near, wide):
    return tuple((source, False, near[n : n + 2], wide[n : n + 2]) for n in (0, 2))


def from_other(where):
    return (where[0], True, *where[2:])


Z_HEAD, Z_TAIL = (0, -1, -2, 1), (-3, 4, 2, 3)
HEAD = (None, False, rows_at(0), column_at(0, Z_HEAD))
LEAD = (None, False, rows_at(-1), column_at(-1, Z_HEAD))
LAG1 = (None, False, rows_at(1), column_at(1, Z_HEAD))
TAIL = (1, False, column_at(0, Z_TAIL), column_at(0, Z_TAIL))
LEAD2 = (None, False, rows_at(-2), column_at(-1, Z_TAIL))
LAG2 = (None, False, rows_at(2), column_at(1, Z_TAIL))
LEAD3 = in_halves(None, rows_at(-3), column_at(2, Z_HEAD))
LAG3 = in_halves(None, rows_at(3), column_at(2, Z_TAIL))
FAR = in_halves(0, rows_at(4), rows_at(4))


def item_of(tick, x):
    return jnp.clip(tick - LAG * x, 0, ITEMS - 1)


def step_kernel(tick, which, meta, consts, env, *refs):
    refs = list(refs)
    arrived = refs.pop(0) if tick >= LAG else None
    both = refs[0]
    e_out, kept, hop, *swaps, current, early = refs[-5 - len(which) :]
    x, zl = meta[0], meta[1]
    turn = tick - LAG * x
    valid = (turn >= 0) & (turn < ITEMS)
    item = item_of(tick, x)
    k, own = lax.rem(item, 4), item // 4
    sec = 2 * zl + own
    target = meta[2 + 4 * k + sec]

    if tick == 0:
        e_out[...] = jnp.zeros_like(e_out)

    @pl.when(x == 0)
    def _():
        current[...] = env[item]

    if tick >= LAG:

        @pl.when(x != 0)
        def _():
            current[...] = arrived[...]

    @pl.when(valid)
    def _():
        def one_site(s, carry):
            if True:
                middle = jnp.dot(current[...], both[s, target, :, :WIDE], preferred_element_type=jnp.float32).astype(jnp.bfloat16)
                total = consts[4 * s + k] * both[s, sec, :, WIDE:].astype(jnp.float32)
                for d in range(LOCAL):
                    cols = slice(d * BLK, (d + 1) * BLK)
                    total += lax.dot_general(both[s, sec, :, cols], middle[:, cols], FIRST_AXES, preferred_element_type=jnp.float32)
                new = total.astype(jnp.bfloat16)
                current[...] = new
                e_out[own, s] += consts[16 + 4 * s + k] * new.astype(jnp.float32)

            @pl.when(s == 1)
            def _():
                early[...] = current[...]

            return carry

        lax.fori_loop(0, 4, one_site, 0)
        hop[...] = current[...]

        @pl.when(zl == 0)
        def _():
            kept[item] = early[...]

        @pl.when(zl == 1)
        def _():
            kept[item] = current[...]

        for part, swap in zip(which, swaps):
            first, end = PARTS[part]
            inside = (item >= first) & (item < end)

            @pl.when(inside & (zl == 0))
            def _():
                swap[item - first] = current[...]

            @pl.when(inside & (zl == 1))
            def _():
                swap[item - first] = early[...]


def parts_at(tick):
    turns = [tick - LAG * x for x in range(NX)]
    return [n for n, (first, end) in enumerate(PARTS) if any(first <= turn < end for turn in turns)]


def step(tick, meta, consts, env, arrived, both, energy, kept, swaps):
    vmem, smem = pl.BlockSpec(memory_space=pltpu.VMEM), pl.BlockSpec(memory_space=pltpu.SMEM)
    which = parts_at(tick)
    operands = [env]
    if tick >= LAG:
        operands.append(arrived)
    operands += [both]
    aliases = {}
    if tick > 0:
        aliases = {2 + len(operands): 0, 3 + len(operands): 1}
        operands += [energy, kept]
    for n, part in enumerate(which):
        if part in swaps:
            aliases[2 + len(operands)] = 3 + n
            operands.append(swaps[part])
    energy, kept, hop, *outs = pl.pallas_call(
        functools.partial(step_kernel, tick, which),
        in_specs=[smem, smem] + [vmem] * len(operands),
        out_specs=(vmem,) * (3 + len(which)),
        out_shape=(
            pltpu.VMEM((2, 4, BLK, BLK), jnp.float32),
            pltpu.VMEM((ITEMS, BLK, BLK), jnp.bfloat16),
            pltpu.VMEM((BLK, BLK), jnp.bfloat16),
        )
        + tuple(pltpu.VMEM((PARTS[n][1] - PARTS[n][0], BLK, BLK), jnp.bfloat16) for n in which),
        scratch_shapes=[pltpu.VMEM((BLK, BLK), jnp.bfloat16)] * 2,
        input_output_aliases=aliases,
        compiler_params=pltpu.CompilerParams(vmem_limit_bytes=STEP_LIMIT),
        name="renormalize",
    )(meta, consts, *[held(v) for v in operands])
    return energy, kept, hop, dict(zip(which, outs))


def place_kernel(part, meta, *refs):
    other, out, sem = refs[0], refs[-2], refs[-1]
    zl = meta[1]
    first, end = PARTS[part]
    copies = []
    for n, item in enumerate(range(first, end)):
        copies.append(pltpu.make_async_copy(other.at[n], out.at[item % 4, 2 * (1 - zl) + item // 4], sem.at[n]))
    if part == 0:
        kept = refs[1]
        for item in range(ITEMS):
            copies.append(pltpu.make_async_copy(kept.at[item], out.at[item % 4, 2 * zl + item // 4], sem.at[ITEMS + item]))
    for copy in copies:
        copy.start()
    for copy in copies:
        copy.wait()


def place_items(part, meta, other, rest):
    vmem, hbm = pl.BlockSpec(memory_space=pltpu.VMEM), pl.BlockSpec(memory_space=pltpu.HBM)
    return pl.pallas_call(
        functools.partial(place_kernel, part),
        in_specs=[pl.BlockSpec(memory_space=pltpu.SMEM), vmem, vmem if part == 0 else hbm],
        out_specs=hbm,
        out_shape=pltpu.HBM((4, SECT, BLK, BLK), jnp.bfloat16),
        scratch_shapes=[pltpu.SemaphoreType.DMA((2 * ITEMS,))],
        input_output_aliases={} if part == 0 else {2: 0},
        compiler_params=pltpu.CompilerParams(vmem_limit_bytes=STEP_LIMIT),
        name="place_items",
    )(meta, other, rest)


def piece(value, axis, place, size):
    return lax.dynamic_slice_in_dim(value, place * size, size, axis)


def on_core(body, place, operands, shapes, out_hbm=False):
    vmem = pl.BlockSpec(memory_space=pltpu.VMEM)
    return pl.pallas_call(
        body,
        in_specs=[pl.BlockSpec(memory_space=pltpu.SMEM)] + [vmem] * len(operands),
        out_specs=(vmem,) * len(shapes),
        out_shape=tuple(jax.ShapeDtypeStruct(shape, dtype) for shape, dtype in shapes),
        compiler_params=pltpu.CompilerParams(vmem_limit_bytes=2 * STEP_LIMIT),
        name=body.__name__,
    )(place, *operands)


HALF, QUARTER = BLK // 2, BLK // 8
AROUND = (2, 1, -1)
ALONG = (4, 3, -3, 2, -2, 1, -1)


def rows_of(place, count):
    return pl.ds(pl.multiple_of(place * count, count), count)


def halve(place, energy, out):
    out[...] = energy[:, :, rows_of(1 - place[2], HALF), :].astype(jnp.bfloat16)


def quarter(place, energy, got, own, *outs):
    own_rows, y = rows_of(place[2], HALF), place[1]

    def total(at):
        first = pl.multiple_of(place[2] * HALF + at * QUARTER, QUARTER)
        return energy[:, :, pl.ds(first, QUARTER), :] + got[:, :, rows_of(at, QUARTER), :].astype(jnp.float32)

    own[...] = total(y)
    for out, step in zip(outs, AROUND):
        out[...] = total(lax.rem(y + NY + step, NY)).astype(jnp.bfloat16)


def by_lane(place, own, first, second, third, mine, near, far):
    zl = place[3]

    def total(lane):
        at = pl.ds(2 * lane, 2)
        return own[:, at] + (first[:, at].astype(jnp.float32) + second[:, at].astype(jnp.float32) + third[:, at].astype(jnp.float32))

    mine[...] = total(zl)
    near[...] = mine[...].astype(jnp.bfloat16)
    far[...] = total(1 - zl).astype(jnp.bfloat16)


def line_up(place, mine, *refs):
    out, zl = refs[-1], place[3]

    def total(parity):
        return sum(ref[...].astype(jnp.float32) for ref, step in zip(refs, ALONG) if step % 2 == parity)

    same, other = mine[...] + total(0), total(1)
    for n in range(2):
        for sector in range(2):
            out[n, 2 * zl + sector] = same[sector, n].astype(jnp.bfloat16)
            out[n, 2 * (1 - zl) + sector] = other[sector, n].astype(jnp.bfloat16)


def join_y(place, own, first, second, third, out):
    out[:, :, rows_of(place[1], QUARTER), :] = own[...]
    for ref, step in zip((first, second, third), AROUND):
        out[:, :, rows_of(lax.rem(place[1] + NY - step, NY), QUARTER), :] = ref[...]


def join_core(place, own, other, out):
    out[:, :, rows_of(place[2], HALF), :] = own[...].astype(jnp.float32)
    out[:, :, rows_of(1 - place[2], HALF), :] = other[...].astype(jnp.float32)


def reduce_energy(energy, place, meta, kept, ended):
    bf16, f32 = jnp.bfloat16, jnp.float32
    energy = held(energy)
    (theirs,) = on_core(halve, place, [energy], [((2, 4, HALF, BLK), bf16)])
    got = other_core(theirs)
    shape = (2, 4, QUARTER, BLK)
    own, *parts = on_core(quarter, place, [energy, got], [(shape, f32)] + [(shape, bf16)] * 3)
    parts = [along_y(part, step) for part, step in zip(parts, AROUND)]
    shape = (2, 2, QUARTER, BLK)
    mine, near, far = on_core(by_lane, place, [own, *parts], [(shape, f32)] + [(shape, bf16)] * 2)
    parts = [along_z(far if step % 2 else near, step) for step in ALONG]
    out = place_items(0, meta, other_lane(ended[0]), kept)
    parts, late, out = lax.optimization_barrier((parts, ended[1], out))
    late = other_lane(late)
    (flat,) = on_core(line_up, place, [mine, *parts], [((2, 4, QUARTER, BLK), bf16)])
    parts = [along_y(flat, step) for step in AROUND]
    parts[-1], late = lax.optimization_barrier((parts[-1], late))
    out = place_items(1, meta, late, out)
    (flat,) = on_core(join_y, place, [flat, *parts], [((2, 4, HALF, BLK), bf16)])
    (flat,) = on_core(join_core, place, [flat, other_core(flat)], [((2, 4, BLK, BLK), f32)])
    return out[None], flat


def pick_kernel(pair_of, coupling, weight, out):
    for s in range(2):
        for k in range(4):
            out[4 * s + k] = coupling[s, pair_of[k]]
            out[8 + 4 * s + k] = weight[s, pair_of[k]]


def pick(pair_of, coupling, weight):
    smem = pl.BlockSpec(memory_space=pltpu.SMEM)
    return pl.pallas_call(
        pick_kernel,
        in_specs=[smem] * 3,
        out_specs=smem,
        out_shape=jax.ShapeDtypeStruct((16,), jnp.float32),
        name="pick",
    )(pair_of, coupling, weight)


def local(environment, rotations, site_terms, pair_of, targets, coupling, energy_coef):
    sweep, op = lax.axis_index("sweep"), lax.axis_index("op")
    x, zl = sweep // 2, sweep % 2
    zh, y, c = op // 8, (op // 2) % 4, op % 2
    z = 2 * zh + zl

    wide = jnp.concatenate([rotations, site_terms], axis=3)
    mine, theirs = wide[c], wide[1 - c]
    got = other_core(theirs)
    block = jnp.where(c == 0, jnp.concatenate([mine, got], axis=1), jnp.concatenate([got, mine], axis=1))
    place = jnp.stack([z, y, c, zl]).astype(jnp.int32)

    def prepare(operands):
        pair_of, targets, coupling, energy_coef, environment = operands
        values = pick(pair_of, coupling, energy_coef).reshape(2, 8)
        got = other_lane(values)
        consts = jnp.where(zl == 0, jnp.concatenate([values, got], axis=1), jnp.concatenate([got, values], axis=1)).reshape(-1)
        meta = jnp.concatenate([jnp.stack([x, zl]).astype(jnp.int32), targets.reshape(-1)])
        env = piece(environment, 1, zl, 2).swapaxes(0, 1).reshape(ITEMS, BLK, BLK)
        return consts, meta, env

    operands = (pair_of, targets, coupling, energy_coef, environment)
    both, (consts, meta, env) = gather_plane(block, place, operands, prepare)

    energy, kept, swaps, hops, ended = None, None, {}, [], {}
    for tick in range(TICKS):
        arrived = hops[tick - LAG] if tick >= LAG else None
        energy, kept, hop, swaps = step(tick, meta, consts, env, arrived, both, energy, kept, swaps)
        hops.append(next_stage(hop) if tick < TICKS - LAG else None)
        for part in swaps:
            if part not in parts_at(tick + 1):
                ended[part] = swaps[part]
    return reduce_energy(energy, place, meta, kept, ended)


def solution(mesh):
    return jax.shard_map(
        local,
        mesh=mesh,
        in_specs=(
            P("op", None, None, None),
            P("sweep", None, "op", None),
            P("sweep", None, "op", None),
            P("op"),
            P("op", None),
            P("sweep", None),
            P("sweep", None),
        ),
        out_specs=(P("sweep", "op", None, None, None), P("sweep", None, None, None)),
        check_vma=False,
    )
```
